32 devices in a mesh: groups: 2 (over x), fsdp: 4 (over y, core), tp: 4 (over z).
Axes of the slice: x: 2, y: 2, z: 4, core: 2. Of those that a mesh axis runs over, the one named last changes fastest.
Arguments:
- hidden: bfloat16 [64, 4, 8192], P(('groups', 'fsdp')), parts along dimension 0, may hold values from -6 to 6
- queries: bfloat16 [64, 4, 8192], P(('groups', 'fsdp'), None, 'tp'), parts along dimension 0, may hold values from -6 to 6
- key_value_weight: bfloat16 [2, 8192, 1024], P(None, None, 'tp'), may hold values from -0.0625 to 0.0625
- adapter_down_weight: bfloat16 [4, 64, 8192], P('groups', None, ('fsdp', 'tp')), parts along dimension 0, may hold values from -0.0625 to 0.0625
- adapter_up_weight: bfloat16 [4, 1024, 64], P('groups', 'tp', 'fsdp'), parts along dimension 0, may hold values from -0.5 to 0.5
- rotated_cache_states: bfloat16 [2, 64, 8, 1536, 128], P(None, ('groups', 'fsdp'), 'tp'), parts along dimension 1, may hold values from -6 to 6
- cache_fill_length: int32 [64], P(('groups', 'fsdp')), parts along dimension 0, may hold values from 1 to 1536, as said below
Outputs:
- new_kv: bfloat16 [2, 64, 4, 1024], P(None, ('groups', 'fsdp'), None, 'tp'), parts along dimension 1
- attended: bfloat16 [64, 4, 8192], P(('groups', 'fsdp'), None, 'tp'), parts along dimension 0
The draws below stay inside these ranges and needn't reach their ends.
There are 2 independent parts, one for each index of `groups`. The reference program is written for one: setup_inputs(seed, part) draws one part's arguments, and reference() takes and returns one part's arrays. A program takes and returns all parts, laid end to end along the dimension named above; an argument that names none is the same for every part. Nothing has to cross between parts.
Inputs may be any that keep to these rules, and one draw needn't show every extreme that they name: `cache_fill_length`: the first row has exactly 1536 filled slots.
All inputs are finite; a program needn't handle non-finite values.
Results may differ from the reference program's by a relative error of at most 0.0071.
Values may be sent and summed in bfloat16 or wider, within the bound.
A program may use at most 128 MiB of HBM per device.

```python
import jax
import jax.numpy as jnp
from jax import lax

MODEL_WIDTH = 8192
HEADS = 64
KV_HEADS = 8
HEAD_DIM = 128
ADAPTER_RANK = 64
STEPS = 4
CACHE = 1536
ROWS = 32
KEY_VALUE_WIDTH = 1024


def draw_cache_fill_length(key, part):
    key = jax.random.fold_in(key, 7)
    lengths = jax.random.randint(key, (ROWS,), 1, CACHE + 1)
    return lengths.at[0].set(CACHE).astype(jnp.int32)


def level_of(rng, extent, cuts, least, high):
    loudness, own = 1.0, jax.random.fold_in(rng, 6)
    for axis_at, shards_of in cuts:
        steps = jnp.exp(jax.random.uniform(jax.random.fold_in(own, axis_at), (shards_of,), jnp.float32, least / len(cuts), high / len(cuts)))
        loudness = loudness * jnp.repeat(steps, extent[axis_at] // shards_of).reshape([-1 if axis == axis_at else 1 for axis in range(len(extent))])
    return loudness


def centred(key, dims, width, limit, cuts=(), kind=jnp.bfloat16):
    drawn = jax.random.normal(key, dims, jnp.float32) * width
    if len(cuts) > 0:
        drawn = level_of(key, dims, cuts, -0.22, 0.18) * drawn
    return jnp.clip(drawn, min=-limit, max=limit).astype(kind)


def setup_inputs(seed: int = 0, part: int = 0) -> dict:
    seeds = jax.random.split(jax.random.key(seed), 8)
    part_keys = jax.random.split(jax.random.fold_in(seeds[7], part), 8)
    return {
        "hidden": centred(part_keys[0], (ROWS, STEPS, MODEL_WIDTH), 1.0, 6.0, ((0, 4),)),
        "queries": centred(part_keys[1], (ROWS, STEPS, HEADS * HEAD_DIM), 1.0, 6.0, ((0, 4), (2, 4))),
        "key_value_weight": centred(seeds[2], (2, MODEL_WIDTH, KEY_VALUE_WIDTH), MODEL_WIDTH ** -0.5, 0.0625, ((2, 4),)),
        "adapter_down_weight": centred(part_keys[3], (2, ADAPTER_RANK, MODEL_WIDTH), MODEL_WIDTH ** -0.5, 0.0625, ((2, 16),)),
        "adapter_up_weight": centred(part_keys[4], (2, KEY_VALUE_WIDTH, ADAPTER_RANK), 0.0625, 0.5, ((1, 4), (2, 4))),
        "rotated_cache_states": centred(part_keys[5], (2, ROWS, KV_HEADS, CACHE, HEAD_DIM), 1.0, 6.0, ((1, 4), (2, 4))),
        "cache_fill_length": draw_cache_fill_length(jax.random.fold_in(jax.random.fold_in(seeds[7], part), 71), part),
    }


adapter_scale = 2.0
rope_theta = 500000.0

def rotate(values, position):
    half_dim = values.shape[-1] // 2
    freqs = rope_theta ** (-2.0 * jnp.arange(half_dim, dtype=jnp.float32) / values.shape[-1])
    angles = position[:, :, None, None] * freqs
    cosine = jnp.cos(angles)
    sine = jnp.sin(angles)
    first = values[..., :half_dim]
    second = values[..., half_dim:]
    return jnp.concatenate([first * cosine - second * sine, second * cosine + first * sine], axis=-1)

def reference(hidden, queries, key_value_weight, adapter_down_weight, adapter_up_weight, rotated_cache_states, cache_fill_length):
    hidden_input = hidden.astype(jnp.float32)
    low_rank_product = jnp.einsum('yao,ieo->iyae', hidden_input, adapter_down_weight.astype(jnp.float32), precision=lax.Precision.HIGHEST)
    base_weight = jnp.einsum('rsd,zdc->zrsc', hidden_input, key_value_weight.astype(jnp.float32), precision=lax.Precision.HIGHEST)
    projected_output = base_weight + adapter_scale * jnp.einsum('lgna,lta->lgnt', low_rank_product, adapter_up_weight.astype(jnp.float32), precision=lax.Precision.HIGHEST)
    position = (cache_fill_length[:, None] + jnp.arange(STEPS, dtype=jnp.int32)[None, :]).astype(jnp.float32)
    keys_new = rotate(projected_output[0].reshape(ROWS, STEPS, KV_HEADS, HEAD_DIM), position).astype(jnp.bfloat16)
    values_new = projected_output[1].reshape(ROWS, STEPS, KV_HEADS, HEAD_DIM).astype(jnp.bfloat16)
    new_kv = jnp.stack([keys_new.reshape(ROWS, STEPS, KEY_VALUE_WIDTH), values_new.reshape(ROWS, STEPS, KEY_VALUE_WIDTH)])
    group = HEADS // KV_HEADS
    qrot = rotate(queries.astype(jnp.float32).reshape(ROWS, STEPS, HEADS, HEAD_DIM), position).astype(jnp.bfloat16)
    qrot = qrot.reshape(ROWS, STEPS, KV_HEADS, group, HEAD_DIM)

    def one_row(items):
        query_row, cache_keys, cache_vals, key_row, val_row, length = items
        qf = query_row.astype(jnp.float32)
        cache_scores = jnp.einsum('skgd,kld->kgsl', qf, cache_keys.astype(jnp.float32)) / jnp.sqrt(jnp.float32(HEAD_DIM))
        new_scores = jnp.einsum('skgd,tkd->kgst', qf, key_row.astype(jnp.float32)) / jnp.sqrt(jnp.float32(HEAD_DIM))
        slot_live = jnp.arange(CACHE, dtype=jnp.int32) < length
        causal = jnp.arange(STEPS)[None, :] <= jnp.arange(STEPS)[:, None]
        cache_scores = jnp.where(slot_live[None, None, None, :], cache_scores, -jnp.inf)
        new_scores = jnp.where(causal[None, None, :, :], new_scores, -jnp.inf)
        scores = jnp.concatenate([cache_scores, new_scores], axis=-1)
        peak = lax.optimization_barrier(jnp.max(scores, axis=-1, keepdims=True))
        expo = jnp.exp(scores - peak)
        weights = (expo / lax.optimization_barrier(jnp.sum(expo, axis=-1, keepdims=True))).astype(jnp.bfloat16).astype(jnp.float32)
        output = jnp.einsum('kgsl,kld->skgd', weights[..., :CACHE], cache_vals.astype(jnp.float32))
        output = output + jnp.einsum('kgst,tkd->skgd', weights[..., CACHE:], val_row.astype(jnp.float32))
        return output.reshape(STEPS, HEADS * HEAD_DIM).astype(jnp.bfloat16)
    attended = lax.map(one_row, (qrot, rotated_cache_states[0], rotated_cache_states[1], keys_new, values_new, cache_fill_length))
    return (new_kv, attended)
```

```python
import functools
import math

import jax
import jax.numpy as jnp
import numpy as np
from jax import lax
from jax.experimental import pallas as pl
from jax.experimental.pallas import tpu as pltpu
from jax.sharding import PartitionSpec as P

adapter_scale = 2.0
rope_theta = 500000.0


def rotate(values, position):
    half_dim = values.shape[-1] // 2
    freqs = rope_theta ** (-2.0 * jnp.arange(half_dim, dtype=jnp.float32) / values.shape[-1])
    angles = position[:, :, None, None] * freqs
    cosine = jnp.cos(angles)
    sine = jnp.sin(angles)
    first = values[..., :half_dim]
    second = values[..., half_dim:]
    return jnp.concatenate(
        [first * cosine - second * sine, second * cosine + first * sine], axis=-1
    )


def cache_part(qrot, rotated_cache_states, cache_fill_length):
    head_dim = qrot.shape[-1]
    scores = jnp.einsum(
        "rskgd,rkld->rkgsl", qrot, rotated_cache_states[0], preferred_element_type=jnp.float32
    )
    scores = scores / jnp.sqrt(jnp.float32(head_dim))
    slot_live = (
        jnp.arange(rotated_cache_states.shape[3], dtype=jnp.int32)[None, :]
        < cache_fill_length[:, None]
    )
    return jnp.where(slot_live[:, None, None, None, :], scores, -jnp.inf)


def on_device_plain(
    hidden,
    queries,
    key_value_weight,
    adapter_down_weight,
    adapter_up_weight,
    rotated_cache_states,
    cache_fill_length,
):
    rows_here = hidden.shape[0]
    steps = hidden.shape[1]
    head_dim = rotated_cache_states.shape[4]
    kv_here = rotated_cache_states.shape[2]
    group = queries.shape[2] // (kv_here * head_dim)
    position = (cache_fill_length[:, None] + jnp.arange(steps, dtype=jnp.int32)[None, :]).astype(
        jnp.float32
    )
    qrot = rotate(
        queries.astype(jnp.float32).reshape(rows_here, steps, kv_here * group, head_dim), position
    ).astype(jnp.bfloat16)
    qrot = qrot.reshape(rows_here, steps, kv_here, group, head_dim)
    up_factor_columns = lax.all_gather(adapter_up_weight, "fsdp", axis=2, tiled=True)
    adapter_update = jnp.einsum(
        "zrd,zcr->zdc",
        lax.all_gather(adapter_down_weight, ("fsdp", "tp"), axis=2, tiled=True),
        up_factor_columns,
        preferred_element_type=jnp.float32,
    )
    merged_weight = key_value_weight.astype(jnp.float32) + adapter_scale * adapter_update
    projected_output = jnp.einsum(
        "rsd,zdc->zrsc", hidden.astype(jnp.float32), merged_weight, precision=lax.Precision.HIGHEST
    )
    cache_scores = cache_part(qrot, rotated_cache_states, cache_fill_length)
    keys_new = rotate(
        projected_output[0].reshape(rows_here, steps, kv_here, head_dim), position
    ).astype(jnp.bfloat16)
    values_new = (
        projected_output[1].reshape(rows_here, steps, kv_here, head_dim).astype(jnp.bfloat16)
    )
    new_kv = jnp.stack(
        [
            keys_new.reshape(rows_here, steps, kv_here * head_dim),
            values_new.reshape(rows_here, steps, kv_here * head_dim),
        ]
    )
    new_scores = jnp.einsum("rskgd,rtkd->rkgst", qrot, keys_new, preferred_element_type=jnp.float32)
    new_scores = new_scores / jnp.sqrt(jnp.float32(head_dim))
    causal = jnp.arange(steps)[None, :] <= jnp.arange(steps)[:, None]
    new_scores = jnp.where(causal[None, None, None, :, :], new_scores, -jnp.inf)
    peak = jnp.maximum(
        jnp.max(cache_scores, axis=-1, keepdims=True), jnp.max(new_scores, axis=-1, keepdims=True)
    )
    cache_expo = jnp.exp(cache_scores - peak)
    new_expo = jnp.exp(new_scores - peak)
    totals = jnp.sum(cache_expo, axis=-1, keepdims=True) + jnp.sum(new_expo, axis=-1, keepdims=True)
    cache_weights = (cache_expo / totals).astype(jnp.bfloat16)
    new_weights = (new_expo / totals).astype(jnp.bfloat16)
    output = jnp.einsum(
        "rkgsl,rkld->rskgd",
        cache_weights,
        rotated_cache_states[1],
        preferred_element_type=jnp.float32,
    )
    output = output + jnp.einsum(
        "rkgst,rtkd->rskgd", new_weights, values_new, preferred_element_type=jnp.float32
    )
    attended = output.reshape(rows_here, steps, kv_here * group * head_dim).astype(jnp.bfloat16)
    return (new_kv, attended)

MESH = pl.DeviceIdType.MESH
W_CHUNKS = 4
NT = (((1,), (1,)), ((), ()))


def dot_nt(a, b):
    return lax.dot_general(a, b, NT, preferred_element_type=jnp.float32)


def dot_nn(a, b):
    return jnp.dot(a, b, preferred_element_type=jnp.float32)


def kernel(
    fill_ref,
    freq_ref,
    hidden_hbm,
    queries_hbm,
    weight_hbm,
    down_hbm,
    up_ref,
    cache_hbm,
    new_kv_ref,
    attended_ref,
    hidden_raw,
    hidden_flat,
    queries_raw,
    weight,
    down,
    up_t,
    low,
    keys,
    values,
    cos_q,
    sin_q,
    q_rot,
    out_acc,
    peak_acc,
    sum_acc,
    in_sem,
    weight_sem,
    key_sem,
    value_sem,
    down_send,
    down_recv,
    up_send,
    up_recv,
    low_send,
    low_recv,
):
    rows, steps, width = hidden_raw.shape
    tokens = rows * steps
    kv_here, slots, head_dim = keys.shape[1], keys.shape[2], keys.shape[3]
    half = head_dim // 2
    group = queries_raw.shape[2] // (kv_here * head_dim)
    per_row = group * steps
    part = down.shape[-1]
    rank_here = up_ref.shape[2]
    tp = low.shape[0]
    f = lax.axis_index("fsdp")
    t = lax.axis_index("tp")
    sibling = f + 1 - 2 * lax.rem(f, 2)
    across = lax.rem(f + 2, 4)
    diagonal = sibling + 2 - 4 * (sibling // 2)
    owners = (f, sibling, across, diagonal)

    hidden_copy = pltpu.make_async_copy(hidden_hbm, hidden_raw, in_sem.at[0])
    hidden_copy.start()
    queries_copy = pltpu.make_async_copy(queries_hbm, queries_raw, in_sem.at[1])
    queries_copy.start()
    down_copy = pltpu.make_async_copy(down_hbm, down.at[0], in_sem.at[2])
    down_copy.start()
    depth = width // W_CHUNKS
    weight_copies = []
    for c in range(W_CHUNKS):
        for z in range(2):
            span = pl.ds(c * depth, depth)
            copy = pltpu.make_async_copy(
                weight_hbm.at[z, span], weight.at[z, span], weight_sem.at[z, c]
            )
            copy.start()
            weight_copies.append(copy)

    @pl.loop(0, rows)
    def _(r):
        pltpu.make_async_copy(cache_hbm.at[0, r], keys.at[r], key_sem.at[r]).start()
        pltpu.make_async_copy(cache_hbm.at[1, r], values.at[r], value_sem.at[r]).start()

    barrier = pltpu.get_barrier_semaphore()
    for peer in owners[1:]:
        pl.semaphore_signal(barrier, inc=1, device_id={"fsdp": peer}, device_id_type=MESH)
    for d in range(1, tp):
        pl.semaphore_signal(
            barrier, inc=1, device_id={"tp": lax.rem(t + d, tp)}, device_id_type=MESH
        )
    pl.semaphore_wait(barrier, 3 + tp - 1)

    def send_down(source, slot, z, peer, sem):
        return pltpu.make_async_remote_copy(
            src_ref=source.at[z],
            dst_ref=down.at[slot, z],
            send_sem=down_send.at[sem, z],
            recv_sem=down_recv.at[sem, z],
            device_id={"fsdp": peer},
            device_id_type=MESH,
        )

    to_across = [send_down(down_hbm, 2, z, across, 1) for z in range(2)]
    to_sibling = [send_down(down_hbm, 1, z, sibling, 0) for z in range(2)]
    forward = [send_down(down.at[2], 3, z, sibling, 2) for z in range(2)]
    for copy in to_across + to_sibling:
        copy.start()

    mine = pl.ds(pl.multiple_of(f * rank_here, rank_here), rank_here)
    eye = (
        lax.broadcasted_iota(jnp.int32, (rank_here, rank_here), 0)
        == lax.broadcasted_iota(jnp.int32, (rank_here, rank_here), 1)
    ).astype(jnp.float32).astype(jnp.bfloat16)
    for z in range(2):
        up_t[z, mine, :] = dot_nt(eye, up_ref[z]).astype(jnp.bfloat16)
    up_copies = []
    for n, peer in enumerate(owners[1:]):
        copy = pltpu.make_async_remote_copy(
            src_ref=up_t.at[:, mine, :],
            dst_ref=up_t.at[:, mine, :],
            send_sem=up_send.at[n],
            recv_sem=up_recv.at[n],
            device_id={"fsdp": peer},
            device_id_type=MESH,
        )
        copy.start()
        up_copies.append(copy)

    lane = lax.broadcasted_iota(jnp.int32, (1, head_dim), 1)
    sign = jnp.where(lane < half, -1.0, 1.0).astype(jnp.float32)
    freq = freq_ref[...]

    def tables(count, each):
        at = lax.broadcasted_iota(jnp.int32, (count, head_dim), 0)
        position = lax.rem(at, steps)
        for r in range(rows):
            position = position + jnp.where(at // each == r, fill_ref[r], 0)
        angle = position.astype(jnp.float32) * freq
        return jnp.cos(angle), jnp.sin(angle) * sign

    cos_all, sin_all = tables(rows * 2 * steps, 2 * steps)
    cos_q[...] = cos_all
    sin_q[...] = sin_all
    cos_k, sin_k = tables(tokens, steps)

    hidden_copy.wait()
    block = 512
    for c in range(width // block):
        span = slice(c * block, (c + 1) * block)
        hidden_flat[:, span] = (
            hidden_raw[:, :, span].astype(jnp.float32).reshape(tokens, block).astype(jnp.bfloat16)
        )

    base = [jnp.zeros((tokens, weight.shape[2]), jnp.float32) for _ in range(2)]
    for c in range(W_CHUNKS):
        for z in range(2):
            weight_copies[c * 2 + z].wait()
            span = slice(c * depth, (c + 1) * depth)
            base[z] = base[z] + dot_nn(hidden_flat[:, span], weight[z, span, :])

    def low_of(slot):
        span = pl.ds(pl.multiple_of((owners[slot] * tp + t) * part, part), part)
        factors = down[slot].reshape(down.shape[1] * down.shape[2], part)
        return dot_nt(hidden_flat[:, span], factors)

    down_copy.wait()
    partial = low_of(0)
    for z in range(2):
        to_sibling[z].wait_recv()
    partial = partial + low_of(1)
    for z in range(2):
        to_across[z].wait_recv()
        forward[z].start()
    partial = partial + low_of(2)
    for z in range(2):
        forward[z].wait_recv()
    partial = partial + low_of(3)
    low[t] = partial
    low_copies = []
    for d in range(1, tp):
        copy = pltpu.make_async_remote_copy(
            src_ref=low.at[t],
            dst_ref=low.at[t],
            send_sem=low_send.at[d - 1],
            recv_sem=low_recv.at[d - 1],
            device_id={"tp": lax.rem(t + d, tp)},
            device_id_type=MESH,
        )
        copy.start()
        low_copies.append(copy)

    queries_copy.wait()
    factor = math.log2(math.e) / math.sqrt(head_dim)
    slot_at = lax.broadcasted_iota(jnp.int32, (per_row, slots), 1)

    @pl.loop(0, rows)
    def _(r):
        table = pl.ds(pl.multiple_of(r * 2 * steps, 2 * steps), 2 * steps)
        cosine = jnp.concatenate([cos_q[table, :]] * (group // 2), axis=0)
        sine = jnp.concatenate([sin_q[table, :]] * (group // 2), axis=0)
        here = pl.ds(pl.multiple_of(r * per_row, per_row), per_row)
        row = queries_raw[r].astype(jnp.float32)
        live = slot_at < fill_ref[r]
        pltpu.make_async_copy(cache_hbm.at[0, r], keys.at[r], key_sem.at[r]).wait()
        pltpu.make_async_copy(cache_hbm.at[1, r], values.at[r], value_sem.at[r]).wait()
        for k in range(kv_here):
            first = k * group
            q = jnp.concatenate(
                [row[:, (first + g) * head_dim : (first + g + 1) * head_dim] for g in range(group)],
                axis=0,
            )
            q = (q * cosine + pltpu.roll(q, half, 1) * sine).astype(jnp.bfloat16)
            q_rot[k, here, :] = q
            scores = jnp.where(live, dot_nt(q, keys[r, k]), -1e30)
            peak = jnp.max(scores, axis=1, keepdims=True)
            expo = jnp.exp2((scores - peak) * factor)
            out_acc[k, here, :] = dot_nn(expo.astype(jnp.bfloat16), values[r, k])
            peak_acc[k, here, :] = jnp.broadcast_to(peak, (per_row, head_dim))
            total = jnp.sum(expo, axis=1, keepdims=True)
            sum_acc[k, here, :] = jnp.broadcast_to(total, (per_row, head_dim))

    for copy in low_copies:
        copy.wait_recv()
    for copy in up_copies:
        copy.wait_recv()
    low_all = low[0]
    for d in range(1, tp):
        low_all = low_all + low[d]
    ranks = up_t.shape[1]
    proj = []
    for z in range(2):
        low_z = low_all[:, z * ranks : (z + 1) * ranks]
        high = low_z.astype(jnp.bfloat16)
        rest = (low_z - high.astype(jnp.float32)).astype(jnp.bfloat16)
        factors = up_t[z]
        update = dot_nn(high, factors) + dot_nn(rest, factors)
        proj.append(base[z] + adapter_scale * update)
    count = rows * per_row
    row_at = lax.broadcasted_iota(jnp.int32, (count, tokens), 0)
    col_at = lax.broadcasted_iota(jnp.int32, (count, tokens), 1)
    seen = (row_at // per_row == col_at // steps) & (
        lax.rem(col_at, steps) <= lax.rem(row_at, steps)
    )
    for k in range(kv_here):
        columns = slice(k * head_dim, (k + 1) * head_dim)
        key = proj[0][:, columns]
        key = key * cos_k + pltpu.roll(key, half, 1) * sin_k
        value = proj[1][:, columns]
        for r in range(rows):
            span = slice(r * steps, (r + 1) * steps)
            new_kv_ref[0, r, :, columns] = key[span].astype(jnp.bfloat16)
            new_kv_ref[1, r, :, columns] = value[span].astype(jnp.bfloat16)
        scores = jnp.where(seen, dot_nt(q_rot[k], key.astype(jnp.bfloat16)), -1e30)
        peak_old = peak_acc[k]
        peak = jnp.maximum(peak_old, jnp.max(scores, axis=1, keepdims=True))
        expo = jnp.exp2((scores - peak[:, :tokens]) * factor)
        keep = jnp.exp2((peak_old - peak) * factor)
        total = sum_acc[k] * keep + jnp.sum(expo, axis=1, keepdims=True)
        output = out_acc[k] * keep + dot_nn(expo.astype(jnp.bfloat16), value.astype(jnp.bfloat16))
        output = output / total
        for r in range(rows):
            for g in range(group):
                at = r * per_row + g * steps
                head = k * group + g
                attended_ref[r, :, head * head_dim : (head + 1) * head_dim] = output[
                    at : at + steps
                ].astype(jnp.bfloat16)

    for copy in to_across + to_sibling + forward + up_copies + low_copies:
        copy.wait_send()


def on_device_kernel(hidden, queries, weight, down, up, cache, fill, tp):
    rows, steps, _ = hidden.shape
    tokens = rows * steps
    kv_here, head_dim = cache.shape[2], cache.shape[4]
    per_row = queries.shape[2] // (kv_here * head_dim) * steps
    freqs = rope_theta ** (-2.0 * (np.arange(head_dim) % (head_dim // 2)) / head_dim)
    freqs = jnp.asarray(freqs[None, :], jnp.float32)
    any_spec = pl.BlockSpec(memory_space=pl.ANY)
    vmem_spec = pl.BlockSpec(memory_space=pltpu.VMEM)
    dma = pltpu.SemaphoreType.DMA
    f32, bf16 = jnp.float32, jnp.bfloat16
    moved = sum(math.prod(a.shape) * 2 for a in (hidden, weight, cache))
    return pl.pallas_call(
        kernel,
        out_shape=(
            jax.ShapeDtypeStruct((2, rows, steps, weight.shape[2]), bf16),
            jax.ShapeDtypeStruct(queries.shape, bf16),
        ),
        in_specs=[
            pl.BlockSpec(memory_space=pltpu.SMEM),
            vmem_spec,
            any_spec,
            any_spec,
            any_spec,
            any_spec,
            vmem_spec,
            any_spec,
        ],
        out_specs=(vmem_spec, vmem_spec),
        scratch_shapes=[
            pltpu.VMEM(hidden.shape, bf16),
            pltpu.VMEM((tokens, hidden.shape[2]), bf16),
            pltpu.VMEM(queries.shape, bf16),
            pltpu.VMEM(weight.shape, bf16),
            pltpu.VMEM((4,) + down.shape, bf16),
            pltpu.VMEM((2, up.shape[2] * 4, up.shape[1]), bf16),
            pltpu.VMEM((tp, tokens, 2 * down.shape[1]), f32),
            pltpu.VMEM(cache.shape[1:], bf16),
            pltpu.VMEM(cache.shape[1:], bf16),
            pltpu.VMEM((rows * 2 * steps, head_dim), f32),
            pltpu.VMEM((rows * 2 * steps, head_dim), f32),
            pltpu.VMEM((kv_here, rows * per_row, head_dim), bf16),
            pltpu.VMEM((kv_here, rows * per_row, head_dim), f32),
            pltpu.VMEM((kv_here, rows * per_row, head_dim), f32),
            pltpu.VMEM((kv_here, rows * per_row, head_dim), f32),
            dma((3,)),
            dma((2, W_CHUNKS)),
            dma((rows,)),
            dma((rows,)),
            dma((3, 2)),
            dma((3, 2)),
            dma((3,)),
            dma((3,)),
            dma((tp - 1,)),
            dma((tp - 1,)),
        ],
        compiler_params=pltpu.CompilerParams(
            collective_id=0, has_side_effects=True, vmem_limit_bytes=48 * 1024 * 1024
        ),
        cost_estimate=pl.CostEstimate(
            flops=700_000_000, bytes_accessed=moved, transcendentals=800_000
        ),
    )(fill, freqs, hidden, queries, weight, down, up, cache)


def on_device(*args, mesh):
    hidden, queries, weight, down, up, cache, _ = args
    fits = (
        mesh.shape["fsdp"] == 4
        and mesh.shape["tp"] > 1
        and down.shape[2] % 512 == 0
        and up.shape[2] % 16 == 0
        and down.shape[1] * 2 == 128
        and hidden.shape[:2] == (8, 4)
    )
    if fits:
        return on_device_kernel(*args, tp=mesh.shape["tp"])
    return on_device_plain(*args)


def solution(mesh):
    return jax.shard_map(
        functools.partial(on_device, mesh=mesh),
        mesh=mesh,
        in_specs=(
            P(("groups", "fsdp"), None, None),
            P(("groups", "fsdp"), None, "tp"),
            P(None, None, "tp"),
            P("groups", None, ("fsdp", "tp")),
            P("groups", "tp", "fsdp"),
            P(None, ("groups", "fsdp"), "tp", None, None),
            P(("groups", "fsdp")),
        ),
        out_specs=(P(None, ("groups", "fsdp"), None, "tp"), P(("groups", "fsdp"), None, "tp")),
        check_vma=False,
    )
```

```python
import functools
import math

import jax
import jax.numpy as jnp
from jax import lax
from jax.experimental import pallas as pl
from jax.experimental.pallas import tpu as pltpu
from jax.sharding import PartitionSpec as P

adapter_scale = 2.0
rope_theta = 500000.0


def rotate(values, position):
    half_dim = values.shape[-1] // 2
    freqs = rope_theta ** (-2.0 * jnp.arange(half_dim, dtype=jnp.float32) / values.shape[-1])
    angles = position[:, :, None, None] * freqs
    cosine = jnp.cos(angles)
    sine = jnp.sin(angles)
    first = values[..., :half_dim]
    second = values[..., half_dim:]
    return jnp.concatenate(
        [first * cosine - second * sine, second * cosine + first * sine], axis=-1
    )


def cache_part(qrot, rotated_cache_states, cache_fill_length):
    head_dim = qrot.shape[-1]
    scores = jnp.einsum(
        "rskgd,rkld->rkgsl", qrot, rotated_cache_states[0], preferred_element_type=jnp.float32
    )
    scores = scores / jnp.sqrt(jnp.float32(head_dim))
    slot_live = (
        jnp.arange(rotated_cache_states.shape[3], dtype=jnp.int32)[None, :]
        < cache_fill_length[:, None]
    )
    return jnp.where(slot_live[:, None, None, None, :], scores, -jnp.inf)


def on_device_plain(
    hidden,
    queries,
    key_value_weight,
    adapter_down_weight,
    adapter_up_weight,
    rotated_cache_states,
    cache_fill_length,
):
    rows_here = hidden.shape[0]
    steps = hidden.shape[1]
    head_dim = rotated_cache_states.shape[4]
    kv_here = rotated_cache_states.shape[2]
    group = queries.shape[2] // (kv_here * head_dim)
    position = (cache_fill_length[:, None] + jnp.arange(steps, dtype=jnp.int32)[None, :]).astype(
        jnp.float32
    )
    qrot = rotate(
        queries.astype(jnp.float32).reshape(rows_here, steps, kv_here * group, head_dim), position
    ).astype(jnp.bfloat16)
    qrot = qrot.reshape(rows_here, steps, kv_here, group, head_dim)
    up_factor_columns = lax.all_gather(adapter_up_weight, "fsdp", axis=2, tiled=True)
    adapter_update = jnp.einsum(
        "zrd,zcr->zdc",
        lax.all_gather(adapter_down_weight, ("fsdp", "tp"), axis=2, tiled=True),
        up_factor_columns,
        preferred_element_type=jnp.float32,
    )
    merged_weight = key_value_weight.astype(jnp.float32) + adapter_scale * adapter_update
    projected_output = jnp.einsum(
        "rsd,zdc->zrsc", hidden.astype(jnp.float32), merged_weight, precision=lax.Precision.HIGHEST
    )
    cache_scores = cache_part(qrot, rotated_cache_states, cache_fill_length)
    keys_new = rotate(
        projected_output[0].reshape(rows_here, steps, kv_here, head_dim), position
    ).astype(jnp.bfloat16)
    values_new = (
        projected_output[1].reshape(rows_here, steps, kv_here, head_dim).astype(jnp.bfloat16)
    )
    new_kv = jnp.stack(
        [
            keys_new.reshape(rows_here, steps, kv_here * head_dim),
            values_new.reshape(rows_here, steps, kv_here * head_dim),
        ]
    )
    new_scores = jnp.einsum("rskgd,rtkd->rkgst", qrot, keys_new, preferred_element_type=jnp.float32)
    new_scores = new_scores / jnp.sqrt(jnp.float32(head_dim))
    causal = jnp.arange(steps)[None, :] <= jnp.arange(steps)[:, None]
    new_scores = jnp.where(causal[None, None, None, :, :], new_scores, -jnp.inf)
    peak = jnp.maximum(
        jnp.max(cache_scores, axis=-1, keepdims=True), jnp.max(new_scores, axis=-1, keepdims=True)
    )
    cache_expo = jnp.exp(cache_scores - peak)
    new_expo = jnp.exp(new_scores - peak)
    totals = jnp.sum(cache_expo, axis=-1, keepdims=True) + jnp.sum(new_expo, axis=-1, keepdims=True)
    cache_weights = (cache_expo / totals).astype(jnp.bfloat16)
    new_weights = (new_expo / totals).astype(jnp.bfloat16)
    output = jnp.einsum(
        "rkgsl,rkld->rskgd",
        cache_weights,
        rotated_cache_states[1],
        preferred_element_type=jnp.float32,
    )
    output = output + jnp.einsum(
        "rkgst,rtkd->rskgd", new_weights, values_new, preferred_element_type=jnp.float32
    )
    attended = output.reshape(rows_here, steps, kv_here * group * head_dim).astype(jnp.bfloat16)
    return (new_kv, attended)

MESH = pl.DeviceIdType.MESH
W_CHUNKS = 4
NT = (((1,), (1,)), ((), ()))


def dot_nt(a, b):
    return lax.dot_general(a, b, NT, preferred_element_type=jnp.float32)


def dot_nn(a, b):
    return jnp.dot(a, b, preferred_element_type=jnp.float32)


def kernel(
    fill_hbm,
    hidden_hbm,
    queries_hbm,
    weight_hbm,
    down_hbm,
    up_hbm,
    cache_hbm,
    new_kv_ref,
    attended_ref,
    fill_ref,
    hidden_raw,
    hidden_flat,
    queries_raw,
    weight,
    down,
    up_t,
    low,
    keys,
    values,
    cos_q,
    sin_q,
    q_rot,
    out_acc,
    peak_acc,
    sum_acc,
    in_sem,
    weight_sem,
    key_sem,
    value_sem,
    down_send,
    down_recv,
    up_send,
    up_recv,
    low_send,
    low_recv,
):
    rows, steps, width = hidden_raw.shape
    tokens = rows * steps
    kv_here, slots, head_dim = keys.shape[1], keys.shape[2], keys.shape[3]
    half = head_dim // 2
    group = queries_raw.shape[2] // (kv_here * head_dim)
    per_row = group * steps
    part = down.shape[-1]
    rank_here = up_hbm.shape[1]
    tp = low.shape[0]
    f = lax.axis_index("fsdp")
    t = lax.axis_index("tp")
    sibling = f + 1 - 2 * lax.rem(f, 2)
    across = lax.rem(f + 2, 4)
    diagonal = sibling + 2 - 4 * (sibling // 2)
    owners = (f, sibling, across, diagonal)

    barrier = pltpu.get_barrier_semaphore()
    for peer in owners[1:]:
        pl.semaphore_signal(barrier, inc=1, device_id={"fsdp": peer}, device_id_type=MESH)
    for d in range(1, tp):
        pl.semaphore_signal(
            barrier, inc=1, device_id={"tp": lax.rem(t + d, tp)}, device_id_type=MESH
        )

    fill_copy = pltpu.make_async_copy(fill_hbm, fill_ref, in_sem.at[3])
    fill_copy.start()
    hidden_copy = pltpu.make_async_copy(hidden_hbm, hidden_raw, in_sem.at[0])
    hidden_copy.start()
    queries_copy = pltpu.make_async_copy(queries_hbm, queries_raw, in_sem.at[1])
    queries_copy.start()
    down_copy = pltpu.make_async_copy(down_hbm, down.at[0], in_sem.at[2])
    down_copy.start()
    mine = pl.ds(pl.multiple_of(f * rank_here, rank_here), rank_here)
    up_copy = pltpu.make_async_copy(up_hbm, up_t.at[:, mine, :], in_sem.at[4])
    up_copy.start()

    def key_copy(r):
        return pltpu.make_async_copy(cache_hbm.at[0, r], keys.at[r], key_sem.at[r])

    def value_copy(r):
        return pltpu.make_async_copy(cache_hbm.at[1, r], values.at[r], value_sem.at[r])

    for r in range(rows // 2):
        key_copy(r).start()
        value_copy(r).start()
    depth = width // W_CHUNKS
    weight_copies = []
    for c in range(W_CHUNKS):
        for z in range(2):
            span = pl.ds(c * depth, depth)
            copy = pltpu.make_async_copy(
                weight_hbm.at[z, span], weight.at[z, span], weight_sem.at[z, c]
            )
            copy.start()
            weight_copies.append(copy)
    for r in range(rows // 2, rows):
        key_copy(r).start()
        value_copy(r).start()

    lane = lax.broadcasted_iota(jnp.int32, (1, head_dim), 1)
    sign = jnp.where(lane < half, -1.0, 1.0).astype(jnp.float32)
    freq = jnp.ones((1, head_dim), jnp.float32)
    for bit in range(half.bit_length() - 1):
        step = rope_theta ** (-2.0 * 2**bit / head_dim)
        freq = jnp.where((lane >> bit) & 1 == 1, freq * step, freq)

    fill_copy.wait()

    def tables(count, each):
        at = lax.broadcasted_iota(jnp.int32, (count, head_dim), 0)
        position = lax.rem(at, steps)
        for r in range(rows):
            position = position + jnp.where(at // each == r, fill_ref[r], 0)
        angle = position.astype(jnp.float32) * freq
        return jnp.cos(angle), jnp.sin(angle) * sign

    cos_all, sin_all = tables(rows * 2 * steps, 2 * steps)
    cos_q[...] = cos_all
    sin_q[...] = sin_all
    cos_k, sin_k = tables(tokens, steps)

    hidden_copy.wait()
    block = 512
    for c in range(width // block):
        span = slice(c * block, (c + 1) * block)
        hidden_flat[:, span] = (
            hidden_raw[:, :, span].astype(jnp.float32).reshape(tokens, block).astype(jnp.bfloat16)
        )

    factor = math.log2(math.e) / math.sqrt(head_dim)
    slot_at = lax.broadcasted_iota(jnp.int32, (1, slots), 1)

    def attend(pair):
        chains = []
        for r in pair:
            table = slice(r * 2 * steps, (r + 1) * 2 * steps)
            cosine = jnp.concatenate([cos_q[table, :]] * (group // 2), axis=0)
            sine = jnp.concatenate([sin_q[table, :]] * (group // 2), axis=0)
            row = queries_raw[r].astype(jnp.float32)
            bias = jnp.where(slot_at < fill_ref[r], 0.0, -1e30)
            for k in range(kv_here):
                heads = range(k * group, (k + 1) * group)
                q = jnp.concatenate(
                    [row[:, h * head_dim : (h + 1) * head_dim] for h in heads], axis=0
                )
                q = (q * cosine + pltpu.roll(q, half, 1) * sine).astype(jnp.bfloat16)
                here = slice(r * per_row, (r + 1) * per_row)
                q_rot[k, here, :] = q
                chains.append((r, k, here, q, bias))
        for r in pair:
            key_copy(r).wait()
            value_copy(r).wait()
        scores = [dot_nt(q, keys[r, k]) + bias for r, k, here, q, bias in chains]
        for (r, k, here, q, bias), score in zip(chains, scores):
            peak = jnp.max(score, axis=1, keepdims=True)
            expo = jnp.exp2((score - peak) * factor)
            out_acc[k, here, :] = dot_nn(expo.astype(jnp.bfloat16), values[r, k])
            peak_acc[k, here, :] = jnp.broadcast_to(peak, (per_row, head_dim))
            total = jnp.sum(expo, axis=1, keepdims=True)
            sum_acc[k, here, :] = jnp.broadcast_to(total, (per_row, head_dim))

    quarter = rows // 4
    queries_copy.wait()
    attend(range(quarter))

    pl.semaphore_wait(barrier, 3 + tp - 1)

    def send_down(source, slot, z, peer, sem):
        return pltpu.make_async_remote_copy(
            src_ref=source.at[z],
            dst_ref=down.at[slot, z],
            send_sem=down_send.at[sem, z],
            recv_sem=down_recv.at[sem, z],
            device_id={"fsdp": peer},
            device_id_type=MESH,
        )

    to_across = [send_down(down_hbm, 2, z, across, 1) for z in range(2)]
    to_sibling = [send_down(down_hbm, 1, z, sibling, 0) for z in range(2)]
    forward = [send_down(down.at[2], 3, z, sibling, 2) for z in range(2)]
    for copy in to_across + to_sibling:
        copy.start()

    up_copies = []
    for n, peer in enumerate(owners[1:]):
        copy = pltpu.make_async_remote_copy(
            src_ref=up_hbm,
            dst_ref=up_t.at[:, mine, :],
            send_sem=up_send.at[n],
            recv_sem=up_recv.at[n],
            device_id={"fsdp": peer},
            device_id_type=MESH,
        )
        copy.start()
        up_copies.append(copy)
    attend(range(quarter, 2 * quarter))

    base = [jnp.zeros((tokens, weight.shape[2]), jnp.float32) for _ in range(2)]
    for c in range(W_CHUNKS):
        for z in range(2):
            weight_copies[c * 2 + z].wait()
            span = slice(c * depth, (c + 1) * depth)
            base[z] = base[z] + dot_nn(hidden_flat[:, span], weight[z, span, :])

    for z in range(2):
        to_across[z].wait_recv()
        forward[z].start()
    attend(range(2 * quarter, 3 * quarter))

    def low_of(slot):
        span = pl.ds(pl.multiple_of((owners[slot] * tp + t) * part, part), part)
        factors = down[slot].reshape(down.shape[1] * down.shape[2], part)
        return dot_nt(hidden_flat[:, span], factors)

    down_copy.wait()
    for copy in to_sibling + forward:
        copy.wait_recv()
    partial = (low_of(0) + low_of(1)) + (low_of(2) + low_of(3))
    low[t] = partial
    low_copies = []
    for d in range(1, tp):
        copy = pltpu.make_async_remote_copy(
            src_ref=low.at[t],
            dst_ref=low.at[t],
            send_sem=low_send.at[d - 1],
            recv_sem=low_recv.at[d - 1],
            device_id={"tp": lax.rem(t + d, tp)},
            device_id_type=MESH,
        )
        copy.start()
        low_copies.append(copy)

    attend(range(3 * quarter, rows))

    for copy in low_copies:
        copy.wait_recv()
    for copy in up_copies:
        copy.wait_recv()
    up_copy.wait()
    low_all = low[0]
    for d in range(1, tp):
        low_all = low_all + low[d]
    ranks = up_t.shape[1]
    proj = []
    for z in range(2):
        low_z = low_all[:, z * ranks : (z + 1) * ranks]
        high = low_z.astype(jnp.bfloat16)
        rest = (low_z - high.astype(jnp.float32)).astype(jnp.bfloat16)
        factors = up_t[z]
        update = dot_nn(high, factors) + dot_nn(rest, factors)
        proj.append(base[z] + adapter_scale * update)
    count = rows * per_row
    row_at = lax.broadcasted_iota(jnp.int32, (count, tokens), 0)
    col_at = lax.broadcasted_iota(jnp.int32, (count, tokens), 1)
    seen = (row_at // per_row == col_at // steps) & (
        lax.rem(col_at, steps) <= lax.rem(row_at, steps)
    )
    for k in range(kv_here):
        columns = slice(k * head_dim, (k + 1) * head_dim)
        key = proj[0][:, columns]
        key = key * cos_k + pltpu.roll(key, half, 1) * sin_k
        value = proj[1][:, columns]
        for r in range(rows):
            span = slice(r * steps, (r + 1) * steps)
            new_kv_ref[0, r, :, columns] = key[span].astype(jnp.bfloat16)
            new_kv_ref[1, r, :, columns] = value[span].astype(jnp.bfloat16)
        scores = jnp.where(seen, dot_nt(q_rot[k], key.astype(jnp.bfloat16)), -1e30)
        peak_old = peak_acc[k]
        peak = jnp.maximum(peak_old, jnp.max(scores, axis=1, keepdims=True))
        expo = jnp.exp2((scores - peak[:, :tokens]) * factor)
        keep = jnp.exp2((peak_old - peak) * factor)
        total = sum_acc[k] * keep + jnp.sum(expo, axis=1, keepdims=True)
        output = out_acc[k] * keep + dot_nn(expo.astype(jnp.bfloat16), value.astype(jnp.bfloat16))
        output = output / total
        for r in range(rows):
            for g in range(group):
                at = r * per_row + g * steps
                head = k * group + g
                attended_ref[r, :, head * head_dim : (head + 1) * head_dim] = output[
                    at : at + steps
                ].astype(jnp.bfloat16)

    for copy in to_across + to_sibling + forward + up_copies + low_copies:
        copy.wait_send()


def on_device_kernel(hidden, queries, weight, down, up, cache, fill, tp):
    rows, steps, _ = hidden.shape
    tokens = rows * steps
    kv_here, head_dim = cache.shape[2], cache.shape[4]
    per_row = queries.shape[2] // (kv_here * head_dim) * steps
    hbm_spec = pl.BlockSpec(memory_space=pltpu.HBM)
    vmem_spec = pl.BlockSpec(memory_space=pltpu.VMEM)
    dma = pltpu.SemaphoreType.DMA
    f32, bf16 = jnp.float32, jnp.bfloat16
    moved = sum(math.prod(a.shape) * 2 for a in (hidden, weight, cache))
    return pl.pallas_call(
        kernel,
        out_shape=(
            jax.ShapeDtypeStruct((2, rows, steps, weight.shape[2]), bf16),
            jax.ShapeDtypeStruct(queries.shape, bf16),
        ),
        in_specs=[hbm_spec] * 7,
        out_specs=(vmem_spec, vmem_spec),
        scratch_shapes=[
            pltpu.SMEM(fill.shape, jnp.int32),
            pltpu.VMEM(hidden.shape, bf16),
            pltpu.VMEM((tokens, hidden.shape[2]), bf16),
            pltpu.VMEM(queries.shape, bf16),
            pltpu.VMEM(weight.shape, bf16),
            pltpu.VMEM((4,) + down.shape, bf16),
            pltpu.VMEM((2, up.shape[2] * 4, up.shape[1]), bf16),
            pltpu.VMEM((tp, tokens, 2 * down.shape[1]), f32),
            pltpu.VMEM(cache.shape[1:], bf16),
            pltpu.VMEM(cache.shape[1:], bf16),
            pltpu.VMEM((rows * 2 * steps, head_dim), f32),
            pltpu.VMEM((rows * 2 * steps, head_dim), f32),
            pltpu.VMEM((kv_here, rows * per_row, head_dim), bf16),
            pltpu.VMEM((kv_here, rows * per_row, head_dim), f32),
            pltpu.VMEM((kv_here, rows * per_row, head_dim), f32),
            pltpu.VMEM((kv_here, rows * per_row, head_dim), f32),
            dma((5,)),
            dma((2, W_CHUNKS)),
            dma((rows,)),
            dma((rows,)),
            dma((3, 2)),
            dma((3, 2)),
            dma((3,)),
            dma((3,)),
            dma((tp - 1,)),
            dma((tp - 1,)),
        ],
        compiler_params=pltpu.CompilerParams(
            collective_id=0, has_side_effects=True, vmem_limit_bytes=64 * 1024 * 1024
        ),
        cost_estimate=pl.CostEstimate(
            flops=700_000_000, bytes_accessed=moved, transcendentals=800_000
        ),
    )(fill, hidden, queries, weight, down, jnp.swapaxes(up, 1, 2), cache)


def on_device(*args, mesh):
    hidden, queries, weight, down, up, cache, _ = args
    fits = (
        mesh.shape["fsdp"] == 4
        and mesh.shape["tp"] > 1
        and down.shape[2] % 512 == 0
        and up.shape[2] % 16 == 0
        and down.shape[1] * 2 == 128
        and hidden.shape[:2] == (8, 4)
    )
    if fits:
        return on_device_kernel(*args, tp=mesh.shape["tp"])
    return on_device_plain(*args)


def solution(mesh):
    return jax.shard_map(
        functools.partial(on_device, mesh=mesh),
        mesh=mesh,
        in_specs=(
            P(("groups", "fsdp"), None, None),
            P(("groups", "fsdp"), None, "tp"),
            P(None, None, "tp"),
            P("groups", None, ("fsdp", "tp")),
            P("groups", "tp", "fsdp"),
            P(None, ("groups", "fsdp"), "tp", None, None),
            P(("groups", "fsdp")),
        ),
        out_specs=(P(None, ("groups", "fsdp"), None, "tp"), P(("groups", "fsdp"), None, "tp")),
        check_vma=False,
    )
```

```python
import functools
import math

import jax
import jax.numpy as jnp
from jax import lax
from jax.experimental import pallas as pl
from jax.experimental.pallas import tpu as pltpu
from jax.sharding import PartitionSpec as P

adapter_scale = 2.0
rope_theta = 500000.0


def rotate(values, position):
    half_dim = values.shape[-1] // 2
    freqs = rope_theta ** (-2.0 * jnp.arange(half_dim, dtype=jnp.float32) / values.shape[-1])
    angles = position[:, :, None, None] * freqs
    cosine = jnp.cos(angles)
    sine = jnp.sin(angles)
    first = values[..., :half_dim]
    second = values[..., half_dim:]
    return jnp.concatenate(
        [first * cosine - second * sine, second * cosine + first * sine], axis=-1
    )


def cache_part(qrot, rotated_cache_states, cache_fill_length):
    head_dim = qrot.shape[-1]
    scores = jnp.einsum(
        "rskgd,rkld->rkgsl", qrot, rotated_cache_states[0], preferred_element_type=jnp.float32
    )
    scores = scores / jnp.sqrt(jnp.float32(head_dim))
    slot_live = (
        jnp.arange(rotated_cache_states.shape[3], dtype=jnp.int32)[None, :]
        < cache_fill_length[:, None]
    )
    return jnp.where(slot_live[:, None, None, None, :], scores, -jnp.inf)


def on_device_plain(
    hidden,
    queries,
    key_value_weight,
    adapter_down_weight,
    adapter_up_weight,
    rotated_cache_states,
    cache_fill_length,
):
    rows_here = hidden.shape[0]
    steps = hidden.shape[1]
    head_dim = rotated_cache_states.shape[4]
    kv_here = rotated_cache_states.shape[2]
    group = queries.shape[2] // (kv_here * head_dim)
    position = (cache_fill_length[:, None] + jnp.arange(steps, dtype=jnp.int32)[None, :]).astype(
        jnp.float32
    )
    qrot = rotate(
        queries.astype(jnp.float32).reshape(rows_here, steps, kv_here * group, head_dim), position
    ).astype(jnp.bfloat16)
    qrot = qrot.reshape(rows_here, steps, kv_here, group, head_dim)
    up_factor_columns = lax.all_gather(adapter_up_weight, "fsdp", axis=2, tiled=True)
    adapter_update = jnp.einsum(
        "zrd,zcr->zdc",
        lax.all_gather(adapter_down_weight, ("fsdp", "tp"), axis=2, tiled=True),
        up_factor_columns,
        preferred_element_type=jnp.float32,
    )
    merged_weight = key_value_weight.astype(jnp.float32) + adapter_scale * adapter_update
    projected_output = jnp.einsum(
        "rsd,zdc->zrsc", hidden.astype(jnp.float32), merged_weight, precision=lax.Precision.HIGHEST
    )
    cache_scores = cache_part(qrot, rotated_cache_states, cache_fill_length)
    keys_new = rotate(
        projected_output[0].reshape(rows_here, steps, kv_here, head_dim), position
    ).astype(jnp.bfloat16)
    values_new = (
        projected_output[1].reshape(rows_here, steps, kv_here, head_dim).astype(jnp.bfloat16)
    )
    new_kv = jnp.stack(
        [
            keys_new.reshape(rows_here, steps, kv_here * head_dim),
            values_new.reshape(rows_here, steps, kv_here * head_dim),
        ]
    )
    new_scores = jnp.einsum("rskgd,rtkd->rkgst", qrot, keys_new, preferred_element_type=jnp.float32)
    new_scores = new_scores / jnp.sqrt(jnp.float32(head_dim))
    causal = jnp.arange(steps)[None, :] <= jnp.arange(steps)[:, None]
    new_scores = jnp.where(causal[None, None, None, :, :], new_scores, -jnp.inf)
    peak = jnp.maximum(
        jnp.max(cache_scores, axis=-1, keepdims=True), jnp.max(new_scores, axis=-1, keepdims=True)
    )
    cache_expo = jnp.exp(cache_scores - peak)
    new_expo = jnp.exp(new_scores - peak)
    totals = jnp.sum(cache_expo, axis=-1, keepdims=True) + jnp.sum(new_expo, axis=-1, keepdims=True)
    cache_weights = (cache_expo / totals).astype(jnp.bfloat16)
    new_weights = (new_expo / totals).astype(jnp.bfloat16)
    output = jnp.einsum(
        "rkgsl,rkld->rskgd",
        cache_weights,
        rotated_cache_states[1],
        preferred_element_type=jnp.float32,
    )
    output = output + jnp.einsum(
        "rkgst,rtkd->rskgd", new_weights, values_new, preferred_element_type=jnp.float32
    )
    attended = output.reshape(rows_here, steps, kv_here * group * head_dim).astype(jnp.bfloat16)
    return (new_kv, attended)

MESH = pl.DeviceIdType.MESH
W_CHUNKS = 4
CACHE_CHUNKS = 4
NT = (((1,), (1,)), ((), ()))


def dot_nt(a, b):
    return lax.dot_general(a, b, NT, preferred_element_type=jnp.float32)


def dot_nn(a, b):
    return jnp.dot(a, b, preferred_element_type=jnp.float32)


def rotation_tables(fill_ref, rows, each, steps, head_dim):
    half = head_dim // 2
    lane = lax.broadcasted_iota(jnp.int32, (1, head_dim), 1)
    sign = jnp.where(lane < half, -1.0, 1.0).astype(jnp.float32)
    freq = jnp.ones((1, head_dim), jnp.float32)
    for bit in range(half.bit_length() - 1):
        step = rope_theta ** (-2.0 * 2**bit / head_dim)
        freq = jnp.where((lane >> bit) & 1 == 1, freq * step, freq)
    at = lax.broadcasted_iota(jnp.int32, (rows * each, head_dim), 0)
    position = lax.rem(at, steps)
    for r in range(rows):
        position = position + jnp.where(at // each == r, fill_ref[r], 0)
    angle = position.astype(jnp.float32) * freq
    return jnp.cos(angle), jnp.sin(angle) * sign


def kernel(
    fill_hbm,
    hidden_hbm,
    weight_hbm,
    down_hbm,
    up_hbm,
    new_hbm,
    fill_ref,
    hidden_raw,
    hidden_flat,
    weight,
    down,
    up_t,
    low,
    new_acc,
    in_sem,
    weight_sem,
    down_send,
    down_recv,
    up_send,
    up_recv,
    low_send,
    low_recv,
    *,
    head_dim,
):
    rows, steps, width = hidden_raw.shape
    tokens = rows * steps
    kv_here = weight.shape[2] // head_dim
    half = head_dim // 2
    part = down.shape[-1]
    rank_here = up_hbm.shape[1]
    tp = low.shape[0]
    f = lax.axis_index("fsdp")
    t = lax.axis_index("tp")
    sibling = f + 1 - 2 * lax.rem(f, 2)
    across = lax.rem(f + 2, 4)
    diagonal = sibling + 2 - 4 * (sibling // 2)
    owners = (f, sibling, across, diagonal)

    barrier = pltpu.get_barrier_semaphore()
    for peer in owners[1:]:
        pl.semaphore_signal(barrier, inc=1, device_id={"fsdp": peer}, device_id_type=MESH)
    for d in range(1, tp):
        pl.semaphore_signal(
            barrier, inc=1, device_id={"tp": lax.rem(t + d, tp)}, device_id_type=MESH
        )

    fill_copy = pltpu.make_async_copy(fill_hbm, fill_ref, in_sem.at[3])
    fill_copy.start()
    hidden_copy = pltpu.make_async_copy(hidden_hbm, hidden_raw, in_sem.at[0])
    hidden_copy.start()
    down_copy = pltpu.make_async_copy(down_hbm, down.at[0], in_sem.at[2])
    down_copy.start()
    mine = pl.ds(pl.multiple_of(f * rank_here, rank_here), rank_here)
    up_copy = pltpu.make_async_copy(up_hbm, up_t.at[:, mine, :], in_sem.at[4])
    up_copy.start()

    depth = width // W_CHUNKS
    weight_copies = []
    for c in range(W_CHUNKS):
        for z in range(2):
            span = pl.ds(c * depth, depth)
            copy = pltpu.make_async_copy(
                weight_hbm.at[z, span], weight.at[z, span], weight_sem.at[z, c]
            )
            copy.start()
            weight_copies.append(copy)
    pl.semaphore_wait(barrier, 3 + tp - 1)

    def send_down(source, slot, z, peer, sem):
        return pltpu.make_async_remote_copy(
            src_ref=source.at[z],
            dst_ref=down.at[slot, z],
            send_sem=down_send.at[sem, z],
            recv_sem=down_recv.at[sem, z],
            device_id={"fsdp": peer},
            device_id_type=MESH,
        )

    to_across = [send_down(down_hbm, 2, z, across, 1) for z in range(2)]
    to_sibling = [send_down(down_hbm, 1, z, sibling, 0) for z in range(2)]
    forward = [send_down(down.at[2], 3, z, sibling, 2) for z in range(2)]
    for copy in to_across + to_sibling:
        copy.start()

    up_copies = []
    for n, peer in enumerate(owners[1:]):
        copy = pltpu.make_async_remote_copy(
            src_ref=up_hbm,
            dst_ref=up_t.at[:, mine, :],
            send_sem=up_send.at[n],
            recv_sem=up_recv.at[n],
            device_id={"fsdp": peer},
            device_id_type=MESH,
        )
        copy.start()
        up_copies.append(copy)
    fill_copy.wait()
    cos_k, sin_k = rotation_tables(fill_ref, rows, steps, steps, head_dim)
    hidden_copy.wait()
    block = 512
    for c in range(width // block):
        span = slice(c * block, (c + 1) * block)
        hidden_flat[:, span] = (
            hidden_raw[:, :, span].astype(jnp.float32).reshape(tokens, block).astype(jnp.bfloat16)
        )
    base = [jnp.zeros((tokens, weight.shape[2]), jnp.float32) for _ in range(2)]
    for c in range(W_CHUNKS):
        for z in range(2):
            weight_copies[c * 2 + z].wait()
            span = slice(c * depth, (c + 1) * depth)
            base[z] = base[z] + dot_nn(hidden_flat[:, span], weight[z, span, :])

    for z in range(2):
        to_across[z].wait_recv()
        forward[z].start()
    def low_of(slot):
        span = pl.ds(pl.multiple_of((owners[slot] * tp + t) * part, part), part)
        factors = down[slot].reshape(down.shape[1] * down.shape[2], part)
        return dot_nt(hidden_flat[:, span], factors)

    down_copy.wait()
    for copy in to_sibling + forward:
        copy.wait_recv()
    partial = (low_of(0) + low_of(1)) + (low_of(2) + low_of(3))
    low[t] = partial
    low_copies = []
    for d in range(1, tp):
        copy = pltpu.make_async_remote_copy(
            src_ref=low.at[t],
            dst_ref=low.at[t],
            send_sem=low_send.at[d - 1],
            recv_sem=low_recv.at[d - 1],
            device_id={"tp": lax.rem(t + d, tp)},
            device_id_type=MESH,
        )
        copy.start()
        low_copies.append(copy)

    for copy in low_copies:
        copy.wait_recv()
    for copy in up_copies:
        copy.wait_recv()
    up_copy.wait()
    low_all = low[0]
    for d in range(1, tp):
        low_all = low_all + low[d]
    ranks = up_t.shape[1]
    proj = []
    for z in range(2):
        low_z = low_all[:, z * ranks : (z + 1) * ranks]
        high = low_z.astype(jnp.bfloat16)
        rest = (low_z - high.astype(jnp.float32)).astype(jnp.bfloat16)
        factors = up_t[z]
        update = dot_nn(high, factors) + dot_nn(rest, factors)
        proj.append(base[z] + adapter_scale * update)
    for k in range(kv_here):
        columns = slice(k * head_dim, (k + 1) * head_dim)
        key = proj[0][:, columns]
        new_acc[0, :, columns] = key * cos_k + pltpu.roll(key, half, 1) * sin_k
    new_acc[1] = proj[1]
    new_copy = pltpu.make_async_copy(new_acc, new_hbm, in_sem.at[5])
    new_copy.start()
    new_copy.wait()
    for copy in to_across + to_sibling + forward + up_copies + low_copies:
        copy.wait_send()


def attention_kernel(
    fill_ref,
    new_hbm,
    queries_hbm,
    cache_hbm,
    new_kv_ref,
    attended_ref,
    new_raw,
    queries_raw,
    keys,
    values,
    cos_q,
    sin_q,
    q_rot,
    out_acc,
    peak_acc,
    sum_acc,
    in_sem,
    key_sem,
    value_sem,
):
    rows, steps = attended_ref.shape[:2]
    tokens = rows * steps
    kv_here, slots, head_dim = keys.shape[1:]
    count = q_rot.shape[1]
    per_row = count // rows
    group = per_row // steps
    half = head_dim // 2
    chunk = slots // CACHE_CHUNKS
    factor = math.log2(math.e) / math.sqrt(head_dim)

    queries_copy = pltpu.make_async_copy(queries_hbm, queries_raw, in_sem.at[0])
    queries_copy.start()

    def chunk_copies(r, c):
        span = pl.ds(c * chunk, chunk)
        return (
            pltpu.make_async_copy(
                cache_hbm.at[0, r, :, span], keys.at[r, :, span], key_sem.at[r, c]
            ),
            pltpu.make_async_copy(
                cache_hbm.at[1, r, :, span], values.at[r, :, span], value_sem.at[r, c]
            ),
        )

    for r in range(rows):
        for c in range(CACHE_CHUNKS):

            @pl.when(c * chunk < fill_ref[r])
            def _():
                for copy in chunk_copies(r, c):
                    copy.start()

    new_copy = pltpu.make_async_copy(new_hbm, new_raw, in_sem.at[1])
    new_copy.start()
    cos_all, sin_all = rotation_tables(fill_ref, rows, 2 * steps, steps, head_dim)
    cos_q[...] = cos_all
    sin_q[...] = sin_all
    queries_copy.wait()
    for r in range(rows):
        table = slice(r * 2 * steps, (r + 1) * 2 * steps)
        cosine = jnp.concatenate([cos_q[table, :]] * (group // 2), axis=0)
        sine = jnp.concatenate([sin_q[table, :]] * (group // 2), axis=0)
        row = queries_raw[r].astype(jnp.float32)
        for k in range(kv_here):
            heads = range(k * group, (k + 1) * group)
            q = jnp.concatenate([row[:, h * head_dim : (h + 1) * head_dim] for h in heads], axis=0)
            q = q * cosine + pltpu.roll(q, half, 1) * sine
            q_rot[k, r * per_row : (r + 1) * per_row, :] = q.astype(jnp.bfloat16)

    @pl.loop(0, rows)
    def _(r):
        filled = fill_ref[r]
        here = pl.ds(pl.multiple_of(r * per_row, per_row), per_row)
        for used in range(1, CACHE_CHUNKS + 1):

            @pl.when(((used - 1) * chunk < filled) & (filled <= used * chunk))
            def _():
                for c in range(used):
                    for copy in chunk_copies(r, c):
                        copy.wait()
                length = used * chunk
                slot_at = lax.broadcasted_iota(jnp.int32, (1, length), 1)
                bias = jnp.where(slot_at < filled, 0.0, -1e30)
                scores = [
                    dot_nt(q_rot[k, here, :], keys[r, k, :length]) + bias for k in range(kv_here)
                ]
                for k, score in enumerate(scores):
                    peak = jnp.max(score, axis=1, keepdims=True)
                    expo = jnp.exp2((score - peak) * factor)
                    out_acc[k, here, :] = dot_nn(expo.astype(jnp.bfloat16), values[r, k, :length])
                    peak_acc[k, here, :] = jnp.broadcast_to(peak, (per_row, head_dim))
                    total = jnp.sum(expo, axis=1, keepdims=True)
                    sum_acc[k, here, :] = jnp.broadcast_to(total, (per_row, head_dim))

    new_copy.wait()
    row_at = lax.broadcasted_iota(jnp.int32, (count, tokens), 0)
    col_at = lax.broadcasted_iota(jnp.int32, (count, tokens), 1)
    seen = (row_at // per_row == col_at // steps) & (
        lax.rem(col_at, steps) <= lax.rem(row_at, steps)
    )
    for k in range(kv_here):
        columns = slice(k * head_dim, (k + 1) * head_dim)
        key = new_raw[0, :, columns]
        value = new_raw[1, :, columns]
        for r in range(rows):
            span = slice(r * steps, (r + 1) * steps)
            new_kv_ref[0, r, :, columns] = key[span].astype(jnp.bfloat16)
            new_kv_ref[1, r, :, columns] = value[span].astype(jnp.bfloat16)
        scores = jnp.where(seen, dot_nt(q_rot[k], key.astype(jnp.bfloat16)), -1e30)
        peak_old = peak_acc[k]
        peak = jnp.maximum(peak_old, jnp.max(scores, axis=1, keepdims=True))
        expo = jnp.exp2((scores - peak[:, :tokens]) * factor)
        keep = jnp.exp2((peak_old - peak) * factor)
        total = sum_acc[k] * keep + jnp.sum(expo, axis=1, keepdims=True)
        output = out_acc[k] * keep + dot_nn(expo.astype(jnp.bfloat16), value.astype(jnp.bfloat16))
        output = output / total
        for r in range(rows):
            for g in range(group):
                at = r * per_row + g * steps
                head = k * group + g
                attended_ref[r, :, head * head_dim : (head + 1) * head_dim] = output[
                    at : at + steps
                ].astype(jnp.bfloat16)


def on_device_kernel(hidden, queries, weight, down, up, cache, fill, tp):
    rows, steps, _ = hidden.shape
    tokens = rows * steps
    kv_here, head_dim = cache.shape[2], cache.shape[4]
    per_row = queries.shape[2] // (kv_here * head_dim) * steps
    hbm_spec = pl.BlockSpec(memory_space=pltpu.HBM)
    vmem_spec = pl.BlockSpec(memory_space=pltpu.VMEM)
    dma = pltpu.SemaphoreType.DMA
    f32, bf16 = jnp.float32, jnp.bfloat16
    moved = sum(math.prod(a.shape) * 2 for a in (hidden, weight))
    held = (kv_here, rows * per_row, head_dim)
    projected = pl.pallas_call(
        functools.partial(kernel, head_dim=head_dim),
        out_shape=jax.ShapeDtypeStruct((2, tokens, weight.shape[2]), f32),
        in_specs=[hbm_spec] * 5,
        out_specs=hbm_spec,
        scratch_shapes=[
            pltpu.SMEM(fill.shape, jnp.int32),
            pltpu.VMEM(hidden.shape, bf16),
            pltpu.VMEM((tokens, hidden.shape[2]), bf16),
            pltpu.VMEM(weight.shape, bf16),
            pltpu.VMEM((4,) + down.shape, bf16),
            pltpu.VMEM((2, up.shape[2] * 4, up.shape[1]), bf16),
            pltpu.VMEM((tp, tokens, 2 * down.shape[1]), f32),
            pltpu.VMEM((2, tokens, weight.shape[2]), f32),
            dma((6,)),
            dma((2, W_CHUNKS)),
            dma((3, 2)),
            dma((3, 2)),
            dma((3,)),
            dma((3,)),
            dma((tp - 1,)),
            dma((tp - 1,)),
        ],
        compiler_params=pltpu.CompilerParams(
            collective_id=0, has_side_effects=True, vmem_limit_bytes=64 * 1024 * 1024
        ),
        cost_estimate=pl.CostEstimate(
            flops=700_000_000, bytes_accessed=moved, transcendentals=800_000
        ),
    )(fill, hidden, weight, down, jnp.swapaxes(up, 1, 2))
    return pl.pallas_call(
        attention_kernel,
        out_shape=(
            jax.ShapeDtypeStruct((2, rows, steps, weight.shape[2]), bf16),
            jax.ShapeDtypeStruct(queries.shape, bf16),
        ),
        in_specs=[pl.BlockSpec(memory_space=pltpu.SMEM)] + [hbm_spec] * 3,
        out_specs=(vmem_spec, vmem_spec),
        scratch_shapes=[
            pltpu.VMEM((2, tokens, weight.shape[2]), f32),
            pltpu.VMEM(queries.shape, bf16),
            pltpu.VMEM(cache.shape[1:], bf16),
            pltpu.VMEM(cache.shape[1:], bf16),
            pltpu.VMEM((rows * 2 * steps, head_dim), f32),
            pltpu.VMEM((rows * 2 * steps, head_dim), f32),
            pltpu.VMEM(held, bf16),
            pltpu.VMEM(held, f32),
            pltpu.VMEM(held, f32),
            pltpu.VMEM(held, f32),
            dma((2,)),
            dma((rows, CACHE_CHUNKS)),
            dma((rows, CACHE_CHUNKS)),
        ],
        compiler_params=pltpu.CompilerParams(vmem_limit_bytes=64 * 1024 * 1024),
    )(fill, projected, queries, cache)


def on_device(*args, mesh):
    hidden, queries, weight, down, up, cache, _ = args
    fits = (
        mesh.shape["fsdp"] == 4
        and mesh.shape["tp"] > 1
        and down.shape[2] % 512 == 0
        and up.shape[2] % 16 == 0
        and down.shape[1] * 2 == 128
        and cache.shape[3] % (16 * CACHE_CHUNKS) == 0
        and hidden.shape[:2] == (8, 4)
    )
    if fits:
        return on_device_kernel(*args, tp=mesh.shape["tp"])
    return on_device_plain(*args)


def solution(mesh):
    return jax.shard_map(
        functools.partial(on_device, mesh=mesh),
        mesh=mesh,
        in_specs=(
            P(("groups", "fsdp"), None, None),
            P(("groups", "fsdp"), None, "tp"),
            P(None, None, "tp"),
            P("groups", None, ("fsdp", "tp")),
            P("groups", "tp", "fsdp"),
            P(None, ("groups", "fsdp"), "tp", None, None),
            P(("groups", "fsdp")),
        ),
        out_specs=(P(None, ("groups", "fsdp"), None, "tp"), P(("groups", "fsdp"), None, "tp")),
        check_vma=False,
    )
```

```python
import functools
import math

import jax
import jax.numpy as jnp
from jax import lax
from jax.experimental import pallas as pl
from jax.experimental.pallas import tpu as pltpu
from jax.sharding import PartitionSpec as P

adapter_scale = 2.0
rope_theta = 500000.0


def rotate(values, position):
    half_dim = values.shape[-1] // 2
    freqs = rope_theta ** (-2.0 * jnp.arange(half_dim, dtype=jnp.float32) / values.shape[-1])
    angles = position[:, :, None, None] * freqs
    cosine = jnp.cos(angles)
    sine = jnp.sin(angles)
    first = values[..., :half_dim]
    second = values[..., half_dim:]
    return jnp.concatenate(
        [first * cosine - second * sine, second * cosine + first * sine], axis=-1
    )


def cache_part(qrot, rotated_cache_states, cache_fill_length):
    head_dim = qrot.shape[-1]
    scores = jnp.einsum(
        "rskgd,rkld->rkgsl", qrot, rotated_cache_states[0], preferred_element_type=jnp.float32
    )
    scores = scores / jnp.sqrt(jnp.float32(head_dim))
    slot_live = (
        jnp.arange(rotated_cache_states.shape[3], dtype=jnp.int32)[None, :]
        < cache_fill_length[:, None]
    )
    return jnp.where(slot_live[:, None, None, None, :], scores, -jnp.inf)


def on_device_plain(
    hidden,
    queries,
    key_value_weight,
    adapter_down_weight,
    adapter_up_weight,
    rotated_cache_states,
    cache_fill_length,
):
    rows_here = hidden.shape[0]
    steps = hidden.shape[1]
    head_dim = rotated_cache_states.shape[4]
    kv_here = rotated_cache_states.shape[2]
    group = queries.shape[2] // (kv_here * head_dim)
    position = (cache_fill_length[:, None] + jnp.arange(steps, dtype=jnp.int32)[None, :]).astype(
        jnp.float32
    )
    qrot = rotate(
        queries.astype(jnp.float32).reshape(rows_here, steps, kv_here * group, head_dim), position
    ).astype(jnp.bfloat16)
    qrot = qrot.reshape(rows_here, steps, kv_here, group, head_dim)
    up_factor_columns = lax.all_gather(adapter_up_weight, "fsdp", axis=2, tiled=True)
    adapter_update = jnp.einsum(
        "zrd,zcr->zdc",
        lax.all_gather(adapter_down_weight, ("fsdp", "tp"), axis=2, tiled=True),
        up_factor_columns,
        preferred_element_type=jnp.float32,
    )
    merged_weight = key_value_weight.astype(jnp.float32) + adapter_scale * adapter_update
    projected_output = jnp.einsum(
        "rsd,zdc->zrsc", hidden.astype(jnp.float32), merged_weight, precision=lax.Precision.HIGHEST
    )
    cache_scores = cache_part(qrot, rotated_cache_states, cache_fill_length)
    keys_new = rotate(
        projected_output[0].reshape(rows_here, steps, kv_here, head_dim), position
    ).astype(jnp.bfloat16)
    values_new = (
        projected_output[1].reshape(rows_here, steps, kv_here, head_dim).astype(jnp.bfloat16)
    )
    new_kv = jnp.stack(
        [
            keys_new.reshape(rows_here, steps, kv_here * head_dim),
            values_new.reshape(rows_here, steps, kv_here * head_dim),
        ]
    )
    new_scores = jnp.einsum("rskgd,rtkd->rkgst", qrot, keys_new, preferred_element_type=jnp.float32)
    new_scores = new_scores / jnp.sqrt(jnp.float32(head_dim))
    causal = jnp.arange(steps)[None, :] <= jnp.arange(steps)[:, None]
    new_scores = jnp.where(causal[None, None, None, :, :], new_scores, -jnp.inf)
    peak = jnp.maximum(
        jnp.max(cache_scores, axis=-1, keepdims=True), jnp.max(new_scores, axis=-1, keepdims=True)
    )
    cache_expo = jnp.exp(cache_scores - peak)
    new_expo = jnp.exp(new_scores - peak)
    totals = jnp.sum(cache_expo, axis=-1, keepdims=True) + jnp.sum(new_expo, axis=-1, keepdims=True)
    cache_weights = (cache_expo / totals).astype(jnp.bfloat16)
    new_weights = (new_expo / totals).astype(jnp.bfloat16)
    output = jnp.einsum(
        "rkgsl,rkld->rskgd",
        cache_weights,
        rotated_cache_states[1],
        preferred_element_type=jnp.float32,
    )
    output = output + jnp.einsum(
        "rkgst,rtkd->rskgd", new_weights, values_new, preferred_element_type=jnp.float32
    )
    attended = output.reshape(rows_here, steps, kv_here * group * head_dim).astype(jnp.bfloat16)
    return (new_kv, attended)

MESH = pl.DeviceIdType.MESH
W_CHUNKS = 4
NT = (((1,), (1,)), ((), ()))


def dot_nt(a, b):
    return lax.dot_general(a, b, NT, preferred_element_type=jnp.float32)


def dot_nn(a, b):
    return jnp.dot(a, b, preferred_element_type=jnp.float32)


def kernel(
    fill_hbm,
    hidden_hbm,
    queries_hbm,
    weight_hbm,
    down_hbm,
    up_hbm,
    cache_hbm,
    new_hbm,
    q_hbm,
    out_hbm,
    peak_hbm,
    sum_hbm,
    fill_ref,
    hidden_raw,
    hidden_flat,
    queries_raw,
    weight,
    down,
    up_t,
    low,
    keys,
    values,
    cos_q,
    sin_q,
    q_rot,
    out_acc,
    peak_acc,
    sum_acc,
    new_acc,
    in_sem,
    weight_sem,
    key_sem,
    value_sem,
    down_send,
    down_recv,
    up_send,
    up_recv,
    low_send,
    low_recv,
    out_sem,
):
    rows, steps, width = hidden_raw.shape
    tokens = rows * steps
    kv_here, slots, head_dim = keys.shape[1], keys.shape[2], keys.shape[3]
    half = head_dim // 2
    group = queries_raw.shape[2] // (kv_here * head_dim)
    per_row = group * steps
    part = down.shape[-1]
    rank_here = up_hbm.shape[1]
    tp = low.shape[0]
    f = lax.axis_index("fsdp")
    t = lax.axis_index("tp")
    sibling = f + 1 - 2 * lax.rem(f, 2)
    across = lax.rem(f + 2, 4)
    diagonal = sibling + 2 - 4 * (sibling // 2)
    owners = (f, sibling, across, diagonal)

    barrier = pltpu.get_barrier_semaphore()
    for peer in owners[1:]:
        pl.semaphore_signal(barrier, inc=1, device_id={"fsdp": peer}, device_id_type=MESH)
    for d in range(1, tp):
        pl.semaphore_signal(
            barrier, inc=1, device_id={"tp": lax.rem(t + d, tp)}, device_id_type=MESH
        )

    fill_copy = pltpu.make_async_copy(fill_hbm, fill_ref, in_sem.at[3])
    fill_copy.start()
    hidden_copy = pltpu.make_async_copy(hidden_hbm, hidden_raw, in_sem.at[0])
    hidden_copy.start()
    queries_copy = pltpu.make_async_copy(queries_hbm, queries_raw, in_sem.at[1])
    queries_copy.start()
    down_copy = pltpu.make_async_copy(down_hbm, down.at[0], in_sem.at[2])
    down_copy.start()
    mine = pl.ds(pl.multiple_of(f * rank_here, rank_here), rank_here)
    up_copy = pltpu.make_async_copy(up_hbm, up_t.at[:, mine, :], in_sem.at[4])
    up_copy.start()

    def key_copy(r):
        return pltpu.make_async_copy(cache_hbm.at[0, r], keys.at[r], key_sem.at[r])

    def value_copy(r):
        return pltpu.make_async_copy(cache_hbm.at[1, r], values.at[r], value_sem.at[r])

    for r in range(rows // 2):
        key_copy(r).start()
        value_copy(r).start()
    depth = width // W_CHUNKS
    weight_copies = []
    for c in range(W_CHUNKS):
        for z in range(2):
            span = pl.ds(c * depth, depth)
            copy = pltpu.make_async_copy(
                weight_hbm.at[z, span], weight.at[z, span], weight_sem.at[z, c]
            )
            copy.start()
            weight_copies.append(copy)
    for r in range(rows // 2, rows):
        key_copy(r).start()
        value_copy(r).start()

    lane = lax.broadcasted_iota(jnp.int32, (1, head_dim), 1)
    sign = jnp.where(lane < half, -1.0, 1.0).astype(jnp.float32)
    freq = jnp.ones((1, head_dim), jnp.float32)
    for bit in range(half.bit_length() - 1):
        step = rope_theta ** (-2.0 * 2**bit / head_dim)
        freq = jnp.where((lane >> bit) & 1 == 1, freq * step, freq)

    fill_copy.wait()

    def tables(count, each):
        at = lax.broadcasted_iota(jnp.int32, (count, head_dim), 0)
        position = lax.rem(at, steps)
        for r in range(rows):
            position = position + jnp.where(at // each == r, fill_ref[r], 0)
        angle = position.astype(jnp.float32) * freq
        return jnp.cos(angle), jnp.sin(angle) * sign

    cos_all, sin_all = tables(rows * 2 * steps, 2 * steps)
    cos_q[...] = cos_all
    sin_q[...] = sin_all
    cos_k, sin_k = tables(tokens, steps)

    hidden_copy.wait()
    block = 512
    for c in range(width // block):
        span = slice(c * block, (c + 1) * block)
        hidden_flat[:, span] = (
            hidden_raw[:, :, span].astype(jnp.float32).reshape(tokens, block).astype(jnp.bfloat16)
        )

    factor = math.log2(math.e) / math.sqrt(head_dim)
    slot_at = lax.broadcasted_iota(jnp.int32, (1, slots), 1)

    out_copies = []

    def attend(pair):
        chains = []
        for r in pair:
            table = slice(r * 2 * steps, (r + 1) * 2 * steps)
            cosine = jnp.concatenate([cos_q[table, :]] * (group // 2), axis=0)
            sine = jnp.concatenate([sin_q[table, :]] * (group // 2), axis=0)
            row = queries_raw[r].astype(jnp.float32)
            bias = jnp.where(slot_at < fill_ref[r], 0.0, -1e30)
            for k in range(kv_here):
                heads = range(k * group, (k + 1) * group)
                q = jnp.concatenate(
                    [row[:, h * head_dim : (h + 1) * head_dim] for h in heads], axis=0
                )
                q = (q * cosine + pltpu.roll(q, half, 1) * sine).astype(jnp.bfloat16)
                here = slice(r * per_row, (r + 1) * per_row)
                q_rot[k, here, :] = q
                chains.append((r, k, here, q, bias))
        for r in pair:
            key_copy(r).wait()
            value_copy(r).wait()
        scores = [dot_nt(q, keys[r, k]) + bias for r, k, here, q, bias in chains]
        for (r, k, here, q, bias), score in zip(chains, scores):
            peak = jnp.max(score, axis=1, keepdims=True)
            expo = jnp.exp2((score - peak) * factor)
            out_acc[k, here, :] = dot_nn(expo.astype(jnp.bfloat16), values[r, k])
            peak_acc[k, here, :] = jnp.broadcast_to(peak, (per_row, head_dim))
            total = jnp.sum(expo, axis=1, keepdims=True)
            sum_acc[k, here, :] = jnp.broadcast_to(total, (per_row, head_dim))
        span = slice(pair[0] * per_row, (pair[-1] + 1) * per_row)
        held = ((q_rot, q_hbm), (out_acc, out_hbm), (peak_acc, peak_hbm), (sum_acc, sum_hbm))
        for n, (source, target) in enumerate(held):
            copy = pltpu.make_async_copy(
                source.at[:, span, :], target.at[:, span, :], out_sem.at[pair[0], n]
            )
            copy.start()
            out_copies.append(copy)

    quarter = rows // 4
    queries_copy.wait()

    pl.semaphore_wait(barrier, 3 + tp - 1)

    def send_down(source, slot, z, peer, sem):
        return pltpu.make_async_remote_copy(
            src_ref=source.at[z],
            dst_ref=down.at[slot, z],
            send_sem=down_send.at[sem, z],
            recv_sem=down_recv.at[sem, z],
            device_id={"fsdp": peer},
            device_id_type=MESH,
        )

    to_across = [send_down(down_hbm, 2, z, across, 1) for z in range(2)]
    to_sibling = [send_down(down_hbm, 1, z, sibling, 0) for z in range(2)]
    forward = [send_down(down.at[2], 3, z, sibling, 2) for z in range(2)]
    for copy in to_across + to_sibling:
        copy.start()

    up_copies = []
    for n, peer in enumerate(owners[1:]):
        copy = pltpu.make_async_remote_copy(
            src_ref=up_hbm,
            dst_ref=up_t.at[:, mine, :],
            send_sem=up_send.at[n],
            recv_sem=up_recv.at[n],
            device_id={"fsdp": peer},
            device_id_type=MESH,
        )
        copy.start()
        up_copies.append(copy)
    attend(range(quarter))
    attend(range(quarter, 2 * quarter))

    base = [jnp.zeros((tokens, weight.shape[2]), jnp.float32) for _ in range(2)]
    for c in range(W_CHUNKS):
        for z in range(2):
            weight_copies[c * 2 + z].wait()
            span = slice(c * depth, (c + 1) * depth)
            base[z] = base[z] + dot_nn(hidden_flat[:, span], weight[z, span, :])

    for z in range(2):
        to_across[z].wait_recv()
        forward[z].start()
    attend(range(2 * quarter, 3 * quarter))

    def low_of(slot):
        span = pl.ds(pl.multiple_of((owners[slot] * tp + t) * part, part), part)
        factors = down[slot].reshape(down.shape[1] * down.shape[2], part)
        return dot_nt(hidden_flat[:, span], factors)

    down_copy.wait()
    for copy in to_sibling + forward:
        copy.wait_recv()
    partial = (low_of(0) + low_of(1)) + (low_of(2) + low_of(3))
    low[t] = partial
    low_copies = []
    for d in range(1, tp):
        copy = pltpu.make_async_remote_copy(
            src_ref=low.at[t],
            dst_ref=low.at[t],
            send_sem=low_send.at[d - 1],
            recv_sem=low_recv.at[d - 1],
            device_id={"tp": lax.rem(t + d, tp)},
            device_id_type=MESH,
        )
        copy.start()
        low_copies.append(copy)

    attend(range(3 * quarter, rows))

    for copy in low_copies:
        copy.wait_recv()
    for copy in up_copies:
        copy.wait_recv()
    up_copy.wait()
    low_all = low[0]
    for d in range(1, tp):
        low_all = low_all + low[d]
    ranks = up_t.shape[1]
    proj = []
    for z in range(2):
        low_z = low_all[:, z * ranks : (z + 1) * ranks]
        high = low_z.astype(jnp.bfloat16)
        rest = (low_z - high.astype(jnp.float32)).astype(jnp.bfloat16)
        factors = up_t[z]
        update = dot_nn(high, factors) + dot_nn(rest, factors)
        proj.append(base[z] + adapter_scale * update)
    for k in range(kv_here):
        columns = slice(k * head_dim, (k + 1) * head_dim)
        key = proj[0][:, columns]
        new_acc[0, :, columns] = key * cos_k + pltpu.roll(key, half, 1) * sin_k
    new_acc[1] = proj[1]
    new_copy = pltpu.make_async_copy(new_acc, new_hbm, in_sem.at[5])
    new_copy.start()
    new_copy.wait()
    for copy in out_copies:
        copy.wait()
    for copy in to_across + to_sibling + forward + up_copies + low_copies:
        copy.wait_send()


def new_token_kernel(new_ref, q_ref, out_ref, peak_ref, sum_ref, new_kv_ref, attended_ref):
    rows, steps = attended_ref.shape[:2]
    tokens = rows * steps
    kv_here, count, head_dim = q_ref.shape
    per_row = count // rows
    group = per_row // steps
    factor = math.log2(math.e) / math.sqrt(head_dim)
    row_at = lax.broadcasted_iota(jnp.int32, (count, tokens), 0)
    col_at = lax.broadcasted_iota(jnp.int32, (count, tokens), 1)
    seen = (row_at // per_row == col_at // steps) & (
        lax.rem(col_at, steps) <= lax.rem(row_at, steps)
    )
    for k in range(kv_here):
        columns = slice(k * head_dim, (k + 1) * head_dim)
        key = new_ref[0, :, columns]
        value = new_ref[1, :, columns]
        for r in range(rows):
            span = slice(r * steps, (r + 1) * steps)
            new_kv_ref[0, r, :, columns] = key[span].astype(jnp.bfloat16)
            new_kv_ref[1, r, :, columns] = value[span].astype(jnp.bfloat16)
        scores = jnp.where(seen, dot_nt(q_ref[k], key.astype(jnp.bfloat16)), -1e30)
        peak_old = peak_ref[k]
        peak = jnp.maximum(peak_old, jnp.max(scores, axis=1, keepdims=True))
        expo = jnp.exp2((scores - peak[:, :tokens]) * factor)
        keep = jnp.exp2((peak_old - peak) * factor)
        total = sum_ref[k] * keep + jnp.sum(expo, axis=1, keepdims=True)
        output = out_ref[k] * keep + dot_nn(expo.astype(jnp.bfloat16), value.astype(jnp.bfloat16))
        output = output / total
        for r in range(rows):
            for g in range(group):
                at = r * per_row + g * steps
                head = k * group + g
                attended_ref[r, :, head * head_dim : (head + 1) * head_dim] = output[
                    at : at + steps
                ].astype(jnp.bfloat16)


def on_device_kernel(hidden, queries, weight, down, up, cache, fill, tp):
    rows, steps, _ = hidden.shape
    tokens = rows * steps
    kv_here, head_dim = cache.shape[2], cache.shape[4]
    per_row = queries.shape[2] // (kv_here * head_dim) * steps
    hbm_spec = pl.BlockSpec(memory_space=pltpu.HBM)
    vmem_spec = pl.BlockSpec(memory_space=pltpu.VMEM)
    dma = pltpu.SemaphoreType.DMA
    f32, bf16 = jnp.float32, jnp.bfloat16
    moved = sum(math.prod(a.shape) * 2 for a in (hidden, weight, cache))
    held = (kv_here, rows * per_row, head_dim)
    middle = pl.pallas_call(
        kernel,
        out_shape=(
            jax.ShapeDtypeStruct((2, tokens, weight.shape[2]), f32),
            jax.ShapeDtypeStruct(held, bf16),
            jax.ShapeDtypeStruct(held, f32),
            jax.ShapeDtypeStruct(held, f32),
            jax.ShapeDtypeStruct(held, f32),
        ),
        in_specs=[hbm_spec] * 7,
        out_specs=(hbm_spec,) * 5,
        scratch_shapes=[
            pltpu.SMEM(fill.shape, jnp.int32),
            pltpu.VMEM(hidden.shape, bf16),
            pltpu.VMEM((tokens, hidden.shape[2]), bf16),
            pltpu.VMEM(queries.shape, bf16),
            pltpu.VMEM(weight.shape, bf16),
            pltpu.VMEM((4,) + down.shape, bf16),
            pltpu.VMEM((2, up.shape[2] * 4, up.shape[1]), bf16),
            pltpu.VMEM((tp, tokens, 2 * down.shape[1]), f32),
            pltpu.VMEM(cache.shape[1:], bf16),
            pltpu.VMEM(cache.shape[1:], bf16),
            pltpu.VMEM((rows * 2 * steps, head_dim), f32),
            pltpu.VMEM((rows * 2 * steps, head_dim), f32),
            pltpu.VMEM(held, bf16),
            pltpu.VMEM(held, f32),
            pltpu.VMEM(held, f32),
            pltpu.VMEM(held, f32),
            pltpu.VMEM((2, tokens, weight.shape[2]), f32),
            dma((6,)),
            dma((2, W_CHUNKS)),
            dma((rows,)),
            dma((rows,)),
            dma((3, 2)),
            dma((3, 2)),
            dma((3,)),
            dma((3,)),
            dma((tp - 1,)),
            dma((tp - 1,)),
            dma((rows, 4)),
        ],
        compiler_params=pltpu.CompilerParams(
            collective_id=0, has_side_effects=True, vmem_limit_bytes=64 * 1024 * 1024
        ),
        cost_estimate=pl.CostEstimate(
            flops=700_000_000, bytes_accessed=moved, transcendentals=800_000
        ),
    )(fill, hidden, queries, weight, down, jnp.swapaxes(up, 1, 2), cache)
    return pl.pallas_call(
        new_token_kernel,
        out_shape=(
            jax.ShapeDtypeStruct((2, rows, steps, weight.shape[2]), bf16),
            jax.ShapeDtypeStruct(queries.shape, bf16),
        ),
        in_specs=[vmem_spec] * 5,
        out_specs=(vmem_spec, vmem_spec),
        compiler_params=pltpu.CompilerParams(vmem_limit_bytes=64 * 1024 * 1024),
    )(*middle)


def on_device(*args, mesh):
    hidden, queries, weight, down, up, cache, _ = args
    fits = (
        mesh.shape["fsdp"] == 4
        and mesh.shape["tp"] > 1
        and down.shape[2] % 512 == 0
        and up.shape[2] % 16 == 0
        and down.shape[1] * 2 == 128
        and hidden.shape[:2] == (8, 4)
    )
    if fits:
        return on_device_kernel(*args, tp=mesh.shape["tp"])
    return on_device_plain(*args)


def solution(mesh):
    return jax.shard_map(
        functools.partial(on_device, mesh=mesh),
        mesh=mesh,
        in_specs=(
            P(("groups", "fsdp"), None, None),
            P(("groups", "fsdp"), None, "tp"),
            P(None, None, "tp"),
            P("groups", None, ("fsdp", "tp")),
            P("groups", "tp", "fsdp"),
            P(None, ("groups", "fsdp"), "tp", None, None),
            P(("groups", "fsdp")),
        ),
        out_specs=(P(None, ("groups", "fsdp"), None, "tp"), P(("groups", "fsdp"), None, "tp")),
        check_vma=False,
    )
```

```python
import functools
import math

import jax
import jax.numpy as jnp
from jax import lax
from jax.experimental import pallas as pl
from jax.experimental.pallas import tpu as pltpu
from jax.sharding import PartitionSpec as P

adapter_scale = 2.0
rope_theta = 500000.0


def rotate(values, position):
    half_dim = values.shape[-1] // 2
    freqs = rope_theta ** (-2.0 * jnp.arange(half_dim, dtype=jnp.float32) / values.shape[-1])
    angles = position[:, :, None, None] * freqs
    cosine = jnp.cos(angles)
    sine = jnp.sin(angles)
    first = values[..., :half_dim]
    second = values[..., half_dim:]
    return jnp.concatenate(
        [first * cosine - second * sine, second * cosine + first * sine], axis=-1
    )


def cache_part(qrot, rotated_cache_states, cache_fill_length):
    head_dim = qrot.shape[-1]
    scores = jnp.einsum(
        "rskgd,rkld->rkgsl", qrot, rotated_cache_states[0], preferred_element_type=jnp.float32
    )
    scores = scores / jnp.sqrt(jnp.float32(head_dim))
    slot_live = (
        jnp.arange(rotated_cache_states.shape[3], dtype=jnp.int32)[None, :]
        < cache_fill_length[:, None]
    )
    return jnp.where(slot_live[:, None, None, None, :], scores, -jnp.inf)


def on_device_plain(
    hidden,
    queries,
    key_value_weight,
    adapter_down_weight,
    adapter_up_weight,
    rotated_cache_states,
    cache_fill_length,
):
    rows_here = hidden.shape[0]
    steps = hidden.shape[1]
    head_dim = rotated_cache_states.shape[4]
    kv_here = rotated_cache_states.shape[2]
    group = queries.shape[2] // (kv_here * head_dim)
    position = (cache_fill_length[:, None] + jnp.arange(steps, dtype=jnp.int32)[None, :]).astype(
        jnp.float32
    )
    qrot = rotate(
        queries.astype(jnp.float32).reshape(rows_here, steps, kv_here * group, head_dim), position
    ).astype(jnp.bfloat16)
    qrot = qrot.reshape(rows_here, steps, kv_here, group, head_dim)
    up_factor_columns = lax.all_gather(adapter_up_weight, "fsdp", axis=2, tiled=True)
    adapter_update = jnp.einsum(
        "zrd,zcr->zdc",
        lax.all_gather(adapter_down_weight, ("fsdp", "tp"), axis=2, tiled=True),
        up_factor_columns,
        preferred_element_type=jnp.float32,
    )
    merged_weight = key_value_weight.astype(jnp.float32) + adapter_scale * adapter_update
    projected_output = jnp.einsum(
        "rsd,zdc->zrsc", hidden.astype(jnp.float32), merged_weight, precision=lax.Precision.HIGHEST
    )
    cache_scores = cache_part(qrot, rotated_cache_states, cache_fill_length)
    keys_new = rotate(
        projected_output[0].reshape(rows_here, steps, kv_here, head_dim), position
    ).astype(jnp.bfloat16)
    values_new = (
        projected_output[1].reshape(rows_here, steps, kv_here, head_dim).astype(jnp.bfloat16)
    )
    new_kv = jnp.stack(
        [
            keys_new.reshape(rows_here, steps, kv_here * head_dim),
            values_new.reshape(rows_here, steps, kv_here * head_dim),
        ]
    )
    new_scores = jnp.einsum("rskgd,rtkd->rkgst", qrot, keys_new, preferred_element_type=jnp.float32)
    new_scores = new_scores / jnp.sqrt(jnp.float32(head_dim))
    causal = jnp.arange(steps)[None, :] <= jnp.arange(steps)[:, None]
    new_scores = jnp.where(causal[None, None, None, :, :], new_scores, -jnp.inf)
    peak = jnp.maximum(
        jnp.max(cache_scores, axis=-1, keepdims=True), jnp.max(new_scores, axis=-1, keepdims=True)
    )
    cache_expo = jnp.exp(cache_scores - peak)
    new_expo = jnp.exp(new_scores - peak)
    totals = jnp.sum(cache_expo, axis=-1, keepdims=True) + jnp.sum(new_expo, axis=-1, keepdims=True)
    cache_weights = (cache_expo / totals).astype(jnp.bfloat16)
    new_weights = (new_expo / totals).astype(jnp.bfloat16)
    output = jnp.einsum(
        "rkgsl,rkld->rskgd",
        cache_weights,
        rotated_cache_states[1],
        preferred_element_type=jnp.float32,
    )
    output = output + jnp.einsum(
        "rkgst,rtkd->rskgd", new_weights, values_new, preferred_element_type=jnp.float32
    )
    attended = output.reshape(rows_here, steps, kv_here * group * head_dim).astype(jnp.bfloat16)
    return (new_kv, attended)

MESH = pl.DeviceIdType.MESH
W_CHUNKS = 4
NT = (((1,), (1,)), ((), ()))


def dot_nt(a, b):
    return lax.dot_general(a, b, NT, preferred_element_type=jnp.float32)


def dot_nn(a, b):
    return jnp.dot(a, b, preferred_element_type=jnp.float32)


def kernel(
    fill_hbm,
    hidden_hbm,
    queries_hbm,
    weight_hbm,
    down_hbm,
    up_hbm,
    cache_hbm,
    new_hbm,
    q_hbm,
    out_hbm,
    peak_hbm,
    sum_hbm,
    fill_ref,
    hidden_raw,
    hidden_flat,
    queries_raw,
    weight,
    down,
    up_t,
    low,
    keys,
    values,
    cos_q,
    sin_q,
    q_rot,
    out_acc,
    peak_acc,
    sum_acc,
    new_acc,
    in_sem,
    weight_sem,
    key_sem,
    value_sem,
    down_send,
    down_recv,
    up_send,
    up_recv,
    low_send,
    low_recv,
    out_sem,
):
    rows, steps, width = hidden_raw.shape
    tokens = rows * steps
    kv_here, slots, head_dim = keys.shape[1], keys.shape[2], keys.shape[3]
    half = head_dim // 2
    group = queries_raw.shape[2] // (kv_here * head_dim)
    per_row = group * steps
    part = down.shape[-1]
    rank_here = up_hbm.shape[1]
    tp = low.shape[0]
    f = lax.axis_index("fsdp")
    t = lax.axis_index("tp")
    sibling = f + 1 - 2 * lax.rem(f, 2)
    across = lax.rem(f + 2, 4)
    diagonal = sibling + 2 - 4 * (sibling // 2)
    owners = (f, sibling, across, diagonal)

    barrier = pltpu.get_barrier_semaphore()
    for peer in owners[1:]:
        pl.semaphore_signal(barrier, inc=1, device_id={"fsdp": peer}, device_id_type=MESH)
    for d in range(1, tp):
        pl.semaphore_signal(
            barrier, inc=1, device_id={"tp": lax.rem(t + d, tp)}, device_id_type=MESH
        )

    fill_copy = pltpu.make_async_copy(fill_hbm, fill_ref, in_sem.at[3])
    fill_copy.start()
    hidden_copy = pltpu.make_async_copy(hidden_hbm, hidden_raw, in_sem.at[0])
    hidden_copy.start()
    queries_copy = pltpu.make_async_copy(queries_hbm, queries_raw, in_sem.at[1])
    queries_copy.start()
    down_copy = pltpu.make_async_copy(down_hbm, down.at[0], in_sem.at[2])
    down_copy.start()
    mine = pl.ds(pl.multiple_of(f * rank_here, rank_here), rank_here)
    up_copy = pltpu.make_async_copy(up_hbm, up_t.at[:, mine, :], in_sem.at[4])
    up_copy.start()

    def key_copy(r):
        return pltpu.make_async_copy(cache_hbm.at[0, r], keys.at[r], key_sem.at[r])

    def value_copy(r):
        return pltpu.make_async_copy(cache_hbm.at[1, r], values.at[r], value_sem.at[r])

    for r in range(rows // 2):
        key_copy(r).start()
        value_copy(r).start()
    depth = width // W_CHUNKS
    weight_copies = []
    for c in range(W_CHUNKS):
        for z in range(2):
            span = pl.ds(c * depth, depth)
            copy = pltpu.make_async_copy(
                weight_hbm.at[z, span], weight.at[z, span], weight_sem.at[z, c]
            )
            copy.start()
            weight_copies.append(copy)
    for r in range(rows // 2, rows):
        key_copy(r).start()
        value_copy(r).start()

    lane = lax.broadcasted_iota(jnp.int32, (1, head_dim), 1)
    sign = jnp.where(lane < half, -1.0, 1.0).astype(jnp.float32)
    freq = jnp.ones((1, head_dim), jnp.float32)
    for bit in range(half.bit_length() - 1):
        step = rope_theta ** (-2.0 * 2**bit / head_dim)
        freq = jnp.where((lane >> bit) & 1 == 1, freq * step, freq)

    fill_copy.wait()

    def tables(count, each):
        at = lax.broadcasted_iota(jnp.int32, (count, head_dim), 0)
        position = lax.rem(at, steps)
        for r in range(rows):
            position = position + jnp.where(at // each == r, fill_ref[r], 0)
        angle = position.astype(jnp.float32) * freq
        return jnp.cos(angle), jnp.sin(angle) * sign

    cos_all, sin_all = tables(rows * 2 * steps, 2 * steps)
    cos_q[...] = cos_all
    sin_q[...] = sin_all
    cos_k, sin_k = tables(tokens, steps)

    hidden_copy.wait()
    block = 512
    for c in range(width // block):
        span = slice(c * block, (c + 1) * block)
        hidden_flat[:, span] = (
            hidden_raw[:, :, span].astype(jnp.float32).reshape(tokens, block).astype(jnp.bfloat16)
        )

    factor = math.log2(math.e) / math.sqrt(head_dim)
    slot_at = lax.broadcasted_iota(jnp.int32, (1, slots), 1)

    out_copies = []

    def attend(pair):
        chains = []
        for r in pair:
            table = slice(r * 2 * steps, (r + 1) * 2 * steps)
            cosine = jnp.concatenate([cos_q[table, :]] * (group // 2), axis=0)
            sine = jnp.concatenate([sin_q[table, :]] * (group // 2), axis=0)
            row = queries_raw[r].astype(jnp.float32)
            bias = jnp.where(slot_at < fill_ref[r], 0.0, -1e30)
            for k in range(kv_here):
                heads = range(k * group, (k + 1) * group)
                q = jnp.concatenate(
                    [row[:, h * head_dim : (h + 1) * head_dim] for h in heads], axis=0
                )
                q = (q * cosine + pltpu.roll(q, half, 1) * sine).astype(jnp.bfloat16)
                here = slice(r * per_row, (r + 1) * per_row)
                q_rot[k, here, :] = q
                chains.append((r, k, here, q, bias))
        for r in pair:
            key_copy(r).wait()
            value_copy(r).wait()
        scores = [dot_nt(q, keys[r, k]) + bias for r, k, here, q, bias in chains]
        for (r, k, here, q, bias), score in zip(chains, scores):
            peak = jnp.max(score, axis=1, keepdims=True)
            expo = jnp.exp2((score - peak) * factor)
            out_acc[k, here, :] = dot_nn(expo.astype(jnp.bfloat16), values[r, k])
            peak_acc[k, here, :] = jnp.broadcast_to(peak, (per_row, head_dim))
            total = jnp.sum(expo, axis=1, keepdims=True)
            sum_acc[k, here, :] = jnp.broadcast_to(total, (per_row, head_dim))
        span = slice(pair[0] * per_row, (pair[-1] + 1) * per_row)
        held = ((q_rot, q_hbm), (out_acc, out_hbm), (peak_acc, peak_hbm), (sum_acc, sum_hbm))
        for n, (source, target) in enumerate(held):
            copy = pltpu.make_async_copy(
                source.at[:, span, :], target.at[:, span, :], out_sem.at[pair[0], n]
            )
            copy.start()
            out_copies.append(copy)

    quarter = rows // 4
    queries_copy.wait()

    pl.semaphore_wait(barrier, 3 + tp - 1)

    def send_down(source, slot, z, peer, sem):
        return pltpu.make_async_remote_copy(
            src_ref=source.at[z],
            dst_ref=down.at[slot, z],
            send_sem=down_send.at[sem, z],
            recv_sem=down_recv.at[sem, z],
            device_id={"fsdp": peer},
            device_id_type=MESH,
        )

    to_across = [send_down(down_hbm, 2, z, across, 1) for z in range(2)]
    to_sibling = [send_down(down_hbm, 1, z, sibling, 0) for z in range(2)]
    forward = [send_down(down.at[2], 3, z, sibling, 2) for z in range(2)]
    for copy in to_across + to_sibling:
        copy.start()

    up_copies = []
    for n, peer in enumerate(owners[1:]):
        copy = pltpu.make_async_remote_copy(
            src_ref=up_hbm,
            dst_ref=up_t.at[:, mine, :],
            send_sem=up_send.at[n],
            recv_sem=up_recv.at[n],
            device_id={"fsdp": peer},
            device_id_type=MESH,
        )
        copy.start()
        up_copies.append(copy)
    attend(range(quarter))
    attend(range(quarter, 2 * quarter))

    for z in range(2):
        to_across[z].wait_recv()
        forward[z].start()
    base = [jnp.zeros((tokens, weight.shape[2]), jnp.float32) for _ in range(2)]
    for c in range(W_CHUNKS):
        for z in range(2):
            weight_copies[c * 2 + z].wait()
            span = slice(c * depth, (c + 1) * depth)
            base[z] = base[z] + dot_nn(hidden_flat[:, span], weight[z, span, :])

    def low_of(slot):
        span = pl.ds(pl.multiple_of((owners[slot] * tp + t) * part, part), part)
        factors = down[slot].reshape(down.shape[1] * down.shape[2], part)
        return dot_nt(hidden_flat[:, span], factors)

    down_copy.wait()
    for copy in to_sibling + forward:
        copy.wait_recv()
    partial = (low_of(0) + low_of(1)) + (low_of(2) + low_of(3))
    low[t] = partial
    low_copies = []
    for d in range(1, tp):
        copy = pltpu.make_async_remote_copy(
            src_ref=low.at[t],
            dst_ref=low.at[t],
            send_sem=low_send.at[d - 1],
            recv_sem=low_recv.at[d - 1],
            device_id={"tp": lax.rem(t + d, tp)},
            device_id_type=MESH,
        )
        copy.start()
        low_copies.append(copy)

    attend(range(2 * quarter, 3 * quarter))
    attend(range(3 * quarter, rows))

    for copy in low_copies:
        copy.wait_recv()
    for copy in up_copies:
        copy.wait_recv()
    up_copy.wait()
    low_all = low[0]
    for d in range(1, tp):
        low_all = low_all + low[d]
    ranks = up_t.shape[1]
    proj = []
    for z in range(2):
        low_z = low_all[:, z * ranks : (z + 1) * ranks]
        high = low_z.astype(jnp.bfloat16)
        rest = (low_z - high.astype(jnp.float32)).astype(jnp.bfloat16)
        factors = up_t[z]
        update = dot_nn(high, factors) + dot_nn(rest, factors)
        proj.append(base[z] + adapter_scale * update)
    for k in range(kv_here):
        columns = slice(k * head_dim, (k + 1) * head_dim)
        key = proj[0][:, columns]
        new_acc[0, :, columns] = key * cos_k + pltpu.roll(key, half, 1) * sin_k
    new_acc[1] = proj[1]
    new_copy = pltpu.make_async_copy(new_acc, new_hbm, in_sem.at[5])
    new_copy.start()
    new_copy.wait()
    for copy in out_copies:
        copy.wait()
    for copy in to_across + to_sibling + forward + up_copies + low_copies:
        copy.wait_send()


def new_token_kernel(new_ref, q_ref, out_ref, peak_ref, sum_ref, new_kv_ref, attended_ref):
    rows, steps = attended_ref.shape[:2]
    tokens = rows * steps
    kv_here, count, head_dim = q_ref.shape
    per_row = count // rows
    group = per_row // steps
    factor = math.log2(math.e) / math.sqrt(head_dim)
    row_at = lax.broadcasted_iota(jnp.int32, (count, tokens), 0)
    col_at = lax.broadcasted_iota(jnp.int32, (count, tokens), 1)
    seen = (row_at // per_row == col_at // steps) & (
        lax.rem(col_at, steps) <= lax.rem(row_at, steps)
    )
    for k in range(kv_here):
        columns = slice(k * head_dim, (k + 1) * head_dim)
        key = new_ref[0, :, columns]
        value = new_ref[1, :, columns]
        for r in range(rows):
            span = slice(r * steps, (r + 1) * steps)
            new_kv_ref[0, r, :, columns] = key[span].astype(jnp.bfloat16)
            new_kv_ref[1, r, :, columns] = value[span].astype(jnp.bfloat16)
        scores = jnp.where(seen, dot_nt(q_ref[k], key.astype(jnp.bfloat16)), -1e30)
        peak_old = peak_ref[k]
        peak = jnp.maximum(peak_old, jnp.max(scores, axis=1, keepdims=True))
        expo = jnp.exp2((scores - peak[:, :tokens]) * factor)
        keep = jnp.exp2((peak_old - peak) * factor)
        total = sum_ref[k] * keep + jnp.sum(expo, axis=1, keepdims=True)
        output = out_ref[k] * keep + dot_nn(expo.astype(jnp.bfloat16), value.astype(jnp.bfloat16))
        output = output / total
        for r in range(rows):
            for g in range(group):
                at = r * per_row + g * steps
                head = k * group + g
                attended_ref[r, :, head * head_dim : (head + 1) * head_dim] = output[
                    at : at + steps
                ].astype(jnp.bfloat16)


def on_device_kernel(hidden, queries, weight, down, up, cache, fill, tp):
    rows, steps, _ = hidden.shape
    tokens = rows * steps
    kv_here, head_dim = cache.shape[2], cache.shape[4]
    per_row = queries.shape[2] // (kv_here * head_dim) * steps
    hbm_spec = pl.BlockSpec(memory_space=pltpu.HBM)
    vmem_spec = pl.BlockSpec(memory_space=pltpu.VMEM)
    dma = pltpu.SemaphoreType.DMA
    f32, bf16 = jnp.float32, jnp.bfloat16
    moved = sum(math.prod(a.shape) * 2 for a in (hidden, weight, cache))
    held = (kv_here, rows * per_row, head_dim)
    middle = pl.pallas_call(
        kernel,
        out_shape=(
            jax.ShapeDtypeStruct((2, tokens, weight.shape[2]), f32),
            jax.ShapeDtypeStruct(held, bf16),
            jax.ShapeDtypeStruct(held, f32),
            jax.ShapeDtypeStruct(held, f32),
            jax.ShapeDtypeStruct(held, f32),
        ),
        in_specs=[hbm_spec] * 7,
        out_specs=(hbm_spec,) * 5,
        scratch_shapes=[
            pltpu.SMEM(fill.shape, jnp.int32),
            pltpu.VMEM(hidden.shape, bf16),
            pltpu.VMEM((tokens, hidden.shape[2]), bf16),
            pltpu.VMEM(queries.shape, bf16),
            pltpu.VMEM(weight.shape, bf16),
            pltpu.VMEM((4,) + down.shape, bf16),
            pltpu.VMEM((2, up.shape[2] * 4, up.shape[1]), bf16),
            pltpu.VMEM((tp, tokens, 2 * down.shape[1]), f32),
            pltpu.VMEM(cache.shape[1:], bf16),
            pltpu.VMEM(cache.shape[1:], bf16),
            pltpu.VMEM((rows * 2 * steps, head_dim), f32),
            pltpu.VMEM((rows * 2 * steps, head_dim), f32),
            pltpu.VMEM(held, bf16),
            pltpu.VMEM(held, f32),
            pltpu.VMEM(held, f32),
            pltpu.VMEM(held, f32),
            pltpu.VMEM((2, tokens, weight.shape[2]), f32),
            dma((6,)),
            dma((2, W_CHUNKS)),
            dma((rows,)),
            dma((rows,)),
            dma((3, 2)),
            dma((3, 2)),
            dma((3,)),
            dma((3,)),
            dma((tp - 1,)),
            dma((tp - 1,)),
            dma((rows, 4)),
        ],
        compiler_params=pltpu.CompilerParams(
            collective_id=0, has_side_effects=True, vmem_limit_bytes=64 * 1024 * 1024
        ),
        cost_estimate=pl.CostEstimate(
            flops=700_000_000, bytes_accessed=moved, transcendentals=800_000
        ),
    )(fill, hidden, queries, weight, down, jnp.swapaxes(up, 1, 2), cache)
    return pl.pallas_call(
        new_token_kernel,
        out_shape=(
            jax.ShapeDtypeStruct((2, rows, steps, weight.shape[2]), bf16),
            jax.ShapeDtypeStruct(queries.shape, bf16),
        ),
        in_specs=[vmem_spec] * 5,
        out_specs=(vmem_spec, vmem_spec),
        compiler_params=pltpu.CompilerParams(vmem_limit_bytes=64 * 1024 * 1024),
    )(*middle)


def on_device(*args, mesh):
    hidden, queries, weight, down, up, cache, _ = args
    fits = (
        mesh.shape["fsdp"] == 4
        and mesh.shape["tp"] > 1
        and down.shape[2] % 512 == 0
        and up.shape[2] % 16 == 0
        and down.shape[1] * 2 == 128
        and hidden.shape[:2] == (8, 4)
    )
    if fits:
        return on_device_kernel(*args, tp=mesh.shape["tp"])
    return on_device_plain(*args)


def solution(mesh):
    return jax.shard_map(
        functools.partial(on_device, mesh=mesh),
        mesh=mesh,
        in_specs=(
            P(("groups", "fsdp"), None, None),
            P(("groups", "fsdp"), None, "tp"),
            P(None, None, "tp"),
            P("groups", None, ("fsdp", "tp")),
            P("groups", "tp", "fsdp"),
            P(None, ("groups", "fsdp"), "tp", None, None),
            P(("groups", "fsdp")),
        ),
        out_specs=(P(None, ("groups", "fsdp"), None, "tp"), P(("groups", "fsdp"), None, "tp")),
        check_vma=False,
    )
```
